512 devices in a mesh: prow: 16 (over y, core), pcol: 32 (over x, z).
Axes of the slice: x: 4, y: 8, z: 8, core: 2. Of those that a mesh axis runs over, the one named last changes fastest.
Arguments:
- matrix: float32 [2, 4096, 3, 8192], P(None, 'prow', None, 'pcol'), may hold values from -6 to 6
- lower_panel: float32 [2, 4096, 8192], P(None, 'prow', 'pcol'), may hold values from -0.375 to 0.375
- inverses: float32 [2, 256, 256], replicated, as said below
- pivots: int32 [2, 256], replicated, may hold values from 0 to 8191, as said below
- panel_owner: int32 [2], replicated, may hold values from 0 to 31, as said below
Outputs:
- updated: float32 [2, 4096, 3, 8192], P(None, 'prow', None, 'pcol')
The draws below stay inside these ranges and needn't reach their ends.
Inputs may be any that keep to these rules, and one draw needn't show every extreme that they name: For step s, pivots[s, i] is either s * 256 + i or a row at or after (s + 1) * 256; the entries of one step all differ. panel_owner[1] is panel_owner[0] + 1 modulo 32, and one of the two is 32 - 1. Each inverses[s] is unit lower triangular.
All inputs are finite; a program needn't handle non-finite values.
Results may differ from the reference program's by a relative error of at most 0.0001.
Values sent between devices are 32-bit elements; how exact they have to be, the bound alone decides.
A program may use at most 64 MiB of HBM per device.

```python
import jax
import jax.numpy as jnp
from jax import lax

NB = 256
RB_DEV = 2
CB_DEV = 3
N_PROW = 16
N_PCOL = 32


def draw_inverses(key, part):
    key = jax.random.fold_in(key, 1)
    strict = 0.06 * jax.random.normal(key, (2, NB, NB), jnp.float32)
    eye_block = jnp.eye(NB, dtype=jnp.float32)[None, :, :]
    return eye_block + jnp.tril(strict, -1)


def draw_pivots(key, part):
    key = jax.random.fold_in(key, 2)
    total_rows = RB_DEV * N_PROW * NB
    positions = jnp.arange(NB, dtype=jnp.int32)
    result = []
    for section in range(2):
        section_key = jax.random.fold_in(key, 10 + section)
        span = total_rows - (section + 1) * NB
        drawn = jax.random.permutation(section_key, span - 1)[:NB - 1].astype(jnp.int32) + (section + 1) * NB
        last_row = jnp.full((1,), total_rows - 1, dtype=jnp.int32)
        order = jnp.concatenate([drawn, last_row])
        keeper = jax.random.randint(jax.random.fold_in(section_key, 5), (NB,), 0, 4) == 0
        keeper = jnp.where(positions == 0, True, keeper)
        keeper = jnp.where(positions == NB - 1, False, keeper)
        itself = section * NB + positions
        result.append(jnp.where(keeper, itself, order))
    return jnp.stack(result).astype(jnp.int32)


def draw_panel_owner(key, part):
    key = jax.random.fold_in(key, 3)
    first = N_PCOL - 2 + jax.random.randint(key, (), 0, 2)
    return jnp.stack([first, (first + 1) % N_PCOL]).astype(jnp.int32)


def steps_of(stream_key, shape, shards, smallest, top_value):
    gain = 1.0
    for axis_at, parts in shards:
        draws = jax.random.uniform(jax.random.fold_in(jax.random.fold_in(stream_key, 6), axis_at), (parts,), jnp.float32, smallest / len(shards), top_value / len(shards))
        gain = gain * jnp.repeat(jnp.exp(draws), shape[axis_at] // parts).reshape((-1,) + (1,) * (len(shape) - 1 - axis_at))
    return gain


def bell_draw(stream_key, dims, spread, most, split=(), kind=jnp.bfloat16):
    values = jax.random.normal(stream_key, dims, jnp.float32) * spread
    if len(split) > 0:
        values = steps_of(stream_key, dims, split, -0.22, 0.18) * values
    return jnp.clip(values, min=-most, max=most).astype(kind)


def setup_inputs(seed: int = 0) -> dict:
    streams_of = jax.random.split(jax.random.key(seed), 6)
    return {
        "matrix": bell_draw(streams_of[0], (RB_DEV, N_PROW * NB, CB_DEV, N_PCOL * NB), 1.0, 6.0, ((1, 16), (3, 32)), jnp.float32),
        "lower_panel": bell_draw(streams_of[1], (RB_DEV, N_PROW * NB, N_PCOL * NB), NB ** -0.5, 0.375, ((1, 16), (2, 32)), jnp.float32),
        "inverses": draw_inverses(jax.random.fold_in(streams_of[5], 71), 0),
        "pivots": draw_pivots(jax.random.fold_in(streams_of[5], 71), 0),
        "panel_owner": draw_panel_owner(jax.random.fold_in(streams_of[5], 71), 0),
    }


def reference(matrix, lower_panel, inverses, pivots, panel_owner):
    total_rows = RB_DEV * N_PROW * NB
    total_cols = CB_DEV * N_PCOL * NB
    current = matrix.reshape(total_rows, total_cols)
    panels = lower_panel.reshape(total_rows, N_PCOL * NB)
    row_ids = jnp.arange(total_rows, dtype=jnp.int32)
    for section in range(2):
        start = section * NB
        offset = (panel_owner[section] * NB).astype(jnp.int32)
        panel = lax.dynamic_slice_in_dim(panels, offset, NB, 1)
        targets = pivots[section]
        top_block = current[start:start + NB]
        picked = current[targets]
        current = current.at[targets].set(top_block)
        upper = jnp.dot(inverses[section], picked, precision=lax.Precision.HIGHEST)
        below = (row_ids >= start + NB)[:, None]
        masked = jnp.where(below, panel, jnp.zeros((), panel.dtype))
        current = current - jnp.dot(masked, upper, precision=lax.Precision.HIGHEST)
        current = current.at[start:start + NB].set(upper)
    return current.reshape(RB_DEV, N_PROW * NB, CB_DEV, N_PCOL * NB)
```

```python
import jax
import jax.numpy as jnp
from jax import lax
from jax.experimental import pallas as pl
from jax.experimental.pallas import tpu as pltpu
from jax.sharding import PartitionSpec as P

MESH = pl.DeviceIdType.MESH
W = 256
KB = 3
NY = 8
SL = 48
HALF = NY * SL
NX, NZ = 4, 8
NQ = NX * NZ
PR = 16
HOLDERS = (30, 31, 0)


def split(x):
    hi = x.astype(jnp.bfloat16)
    return hi, (x - hi.astype(jnp.float32)).astype(jnp.bfloat16)


def dot(a, b, ca, cb):
    return lax.dot_general(a, b, (((ca,), (cb,)), ((), ())), preferred_element_type=jnp.float32)


def kernel(a_hbm, l_hbm, inv_ref, piv_ref, own_ref, o_hbm, a, loc, pt, pair, s_buf, f_buf, b_buf, r_buf, ut, tt, tsrc,
           lp, lg, o_buf, load_sem, out_sem, pair_s, pair_r, rs_s, rs_r, ts_s, ts_r, ag_s, ag_r, fw_s, fw_r,
           sc_s, sc_r, z_s, z_r, x_s, x_r):
    p, q = lax.axis_index("prow"), lax.axis_index("pcol")
    y, c = p // 2, p % 2
    x, z = q // NZ, q % NZ
    side = 1 - 2 * c

    def at_y(step):
        return (lax.rem(y + step + 2 * NY, NY) * 2 + c, q)

    def chip(step):
        return lax.rem(y + step + 2 * NY, NY)

    mate = (y * 2 + 1 - c, q)

    def at_x(step):
        return (p, lax.rem(x + step, NX) * NZ + z)

    def at_z(step):
        return (p, x * NZ + lax.rem(z + step, NZ))

    sent = []

    def send(src, dst, s, r, to):
        copy = pltpu.make_async_remote_copy(src_ref=src, dst_ref=dst, send_sem=s, recv_sem=r, device_id=to,
                                            device_id_type=MESH)
        copy.start()
        sent.append(copy)
        return copy

    load_a = pltpu.make_async_copy(a_hbm, a, load_sem.at[0])
    load_l = pltpu.make_async_copy(l_hbm, loc, load_sem.at[1])
    load_a.start()
    load_l.start()

    barrier = pltpu.get_barrier_semaphore()
    greet = [at_y(i) for i in range(1, NY)] + [mate] + [at_z(i) for i in range(1, NZ)] + [at_x(i) for i in range(1, NX)]
    for to in greet:
        pl.semaphore_signal(barrier, inc=1, device_id=to, device_id_type=MESH)
    for h in HOLDERS:
        @pl.when(q != h)
        def _():
            pl.semaphore_signal(barrier, inc=1, device_id=(p, h), device_id_type=MESH)

    @pl.when(y != 0)
    def _():
        pl.semaphore_signal(barrier, inc=1, device_id=(1 - c, q), device_id_type=MESH)

    def onehot(s, j):
        rows = lax.broadcasted_iota(jnp.int32, (W, W), 0) + (j * 2 * NY + p) * W
        return rows == piv_ref[s:s + 1, :]

    def offer(s):
        hot = [jnp.where(onehot(s, j), 1.0, 0.0).astype(jnp.bfloat16) for j in range(2)]
        for k in range(KB):
            total = jnp.zeros((W, W), jnp.float32)
            for j in range(2):
                for part in split(a[j, k]):
                    total = total + dot(part, hot[j], 0, 0)
            pt[s, k * W:(k + 1) * W, :] = total

    load_a.wait()
    offer(0)

    holds = jnp.logical_or(q == HOLDERS[0], jnp.logical_or(q == HOLDERS[1], q == HOLDERS[2]))
    heard = len(greet) + jnp.where(holds, NQ - 1, 0) + jnp.where(y == 0, NY - 1, 0)
    pl.semaphore_wait(barrier, heard)

    load_l.wait()
    mine = pl.multiple_of(c * HALF, 8)
    other = pl.multiple_of((1 - c) * HALF, 8)

    def rows_of(step):
        return pl.ds(pl.multiple_of(c * HALF + chip(step) * SL, 8), SL)

    def gather_near(buf, i):
        here = buf.at[rows_of(0)]
        return {st: send(here, here, ag_s.at[i, n], ag_r.at[i, n], at_y(st)) for n, st in enumerate((1, -1, 2, -2))}

    def gather_far(buf, i, near):
        far = []
        near[2].wait_recv()
        from_low = buf.at[rows_of(-2)]
        far.append(send(from_low, from_low, ag_s.at[i, 4], ag_r.at[i, 4], at_y(1)))
        near[-2].wait_recv()
        from_high = buf.at[rows_of(2)]
        far.append(send(from_high, from_high, ag_s.at[i, 5], ag_r.at[i, 5], at_y(-1)))
        across = buf.at[rows_of(-2 * side)]
        far.append(send(across, across, ag_s.at[i, 6], ag_r.at[i, 6], at_y(2 * side)))
        return far

    def share(buf, i, near, far):
        moves = []

        def move(n, step):
            piece = buf.at[rows_of(step)]
            moves.append(send(piece, piece, fw_s.at[i, n], fw_r.at[i, n], mate))

        move(0, 0)
        move(1, 2)
        move(2, -2)
        near[1].wait_recv()
        move(3, -1)
        near[-1].wait_recv()
        move(4, 1)
        far[0].wait_recv()
        move(5, -3)
        far[1].wait_recv()
        move(6, 3)
        far[2].wait_recv()
        move(7, 4)
        return moves

    for s in range(2):
        if s == 1:
            offer(1)
        pair_copy = send(pt.at[s, pl.ds(other, HALF)], pair.at[s], pair_s.at[s], pair_r.at[s], mate)

        @pl.when(p == s)
        def _():
            for k in range(KB):
                tsrc[s, k * W:(k + 1) * W, :] = a[0, k].T
            for t in range(2 * NY):
                piece = pl.ds((t % 2) * HALF + (t // 2) * SL, SL)
                if t == s:
                    tt[s, piece, :] = tsrc[s, piece, :]
                else:
                    pltpu.make_async_remote_copy(src_ref=tsrc.at[s, piece], dst_ref=tt.at[s, piece],
                                                 send_sem=ts_s.at[s, t], recv_sem=ts_r.at[s], device_id=(t, q),
                                                 device_id_type=MESH).start()

        if s == 0:
            for n, h in enumerate(HOLDERS):
                @pl.when(q == h)
                def _():
                    lp[n] = loc[h * PR:(h + 1) * PR, :]

                    @pl.loop(1, NQ)
                    def _(i):
                        to = lax.rem(h + i, NQ)
                        piece = pl.ds(pl.multiple_of(to * PR, 8), PR)
                        pltpu.make_async_remote_copy(src_ref=loc.at[piece], dst_ref=lp.at[n], send_sem=sc_s.at[i],
                                                     recv_sem=sc_r.at[n], device_id=(p, to),
                                                     device_id_type=MESH).start()

        pair_copy.wait_recv()
        for i in range(NY):
            s_buf[s, i] = pt[s, pl.ds(pl.multiple_of(mine + i * SL, 8), SL), :] + pair[s, i * SL:(i + 1) * SL, :]

        far = [
            send(s_buf.at[s, chip(-3)], f_buf.at[s, 0], rs_s.at[s, 0], rs_r.at[s, 0], at_y(-1)),
            send(s_buf.at[s, chip(4)], f_buf.at[s, 1], rs_s.at[s, 1], rs_r.at[s, 1], at_y(-2 * side)),
            send(s_buf.at[s, chip(3)], f_buf.at[s, 2], rs_s.at[s, 2], rs_r.at[s, 2], at_y(1)),
        ]
        near = [
            send(s_buf.at[s, chip(1)], r_buf.at[s, 0], rs_s.at[s, 3], rs_r.at[s, 3], at_y(1)),
            send(s_buf.at[s, chip(-1)], r_buf.at[s, 1], rs_s.at[s, 4], rs_r.at[s, 4], at_y(-1)),
        ]
        for copy in far:
            copy.wait_recv()
        cross = f_buf[s, 1]
        b_buf[s, 0] = s_buf[s, chip(-2)] + f_buf[s, 0] + jnp.where(c == 0, cross, 0.0)
        b_buf[s, 1] = s_buf[s, chip(2)] + f_buf[s, 2] + jnp.where(c == 0, 0.0, cross)
        near += [
            send(b_buf.at[s, 0], r_buf.at[s, 2], rs_s.at[s, 5], rs_r.at[s, 5], at_y(-2)),
            send(b_buf.at[s, 1], r_buf.at[s, 3], rs_s.at[s, 6], rs_r.at[s, 6], at_y(2)),
        ]

        t_here = tt.at[s, rows_of(0)]

        @pl.when(p != s)
        def _():
            pltpu.make_async_remote_copy(src_ref=t_here, dst_ref=t_here, send_sem=ts_s.at[s, 0], recv_sem=ts_r.at[s],
                                         device_id=mate, device_id_type=MESH).wait_recv()
        t_near = gather_near(tt.at[s], 2 * s)

        if s == 0:
            for n, h in enumerate(HOLDERS):
                @pl.when(q != h)
                def _():
                    pltpu.make_async_remote_copy(src_ref=lp.at[n], dst_ref=lp.at[n], send_sem=sc_s.at[0],
                                                 recv_sem=sc_r.at[n], device_id=mate, device_id_type=MESH).wait_recv()
            piece = pl.ds(pl.multiple_of(q * PR, 8), PR)
            for i in range(2):
                chosen = jnp.where(own_ref[i] == HOLDERS[1], lp[1], jnp.where(own_ref[i] == HOLDERS[0], lp[0], lp[2]))
                lg[i, piece, :] = chosen
            z_copies = [send(lg.at[:, piece], lg.at[:, piece], z_s.at[i], z_r.at[i], at_z(i)) for i in range(1, NZ)]

        for copy in near:
            copy.wait_recv()
        total = s_buf[s, y] + r_buf[s, 0] + r_buf[s, 1] + r_buf[s, 2] + r_buf[s, 3]
        ut[s, rows_of(0), :] = lax.dot_general(total, inv_ref[s], (((1,), (1,)), ((), ())),
                                               precision=lax.Precision.HIGHEST, preferred_element_type=jnp.float32)
        u_near = gather_near(ut.at[s], 2 * s + 1)
        t_far = gather_far(tt.at[s], 2 * s, t_near)

        if s == 0:
            for copy in z_copies:
                copy.wait_recv()
            wide = pl.ds(pl.multiple_of(x * (NZ * PR), 8), NZ * PR)
            x_copies = [[send(lg.at[i, wide], lg.at[i, wide], x_s.at[i, n], x_r.at[i, n], at_x(n))
                         for n in range(1, NX)] for i in range(2)]

        u_far = gather_far(ut.at[s], 2 * s + 1, u_near)
        moves = share(tt.at[s], 2 * s, t_near, t_far)
        moves += share(ut.at[s], 2 * s + 1, u_near, u_far)
        for copy in moves:
            copy.wait_recv()
        for copy in x_copies[s]:
            copy.wait_recv()

        hot = [onehot(s, j) for j in range(2)]
        taken = [jnp.sum(jnp.where(h, 1.0, 0.0), axis=1, keepdims=True) > 0.0 for h in hot]
        hot = [jnp.where(h, 1.0, 0.0).astype(jnp.bfloat16) for h in hot]
        low = [jnp.where(p > s, lg[s, :W, :], 0.0), lg[s, W:, :]]
        low = [split(v) for v in low]
        out = a if s == 0 else o_buf
        for k in range(KB):
            cols = pl.ds(k * W, W)
            t_parts = split(tt[s, cols, :])
            u_parts = split(ut[s, cols, :])
            for j in range(2):
                swapped = dot(hot[j], t_parts[0], 1, 1) + dot(hot[j], t_parts[1], 1, 1)
                base = jnp.where(taken[j], swapped, a[j, k])
                product = (dot(low[j][0], u_parts[0], 1, 1) + dot(low[j][0], u_parts[1], 1, 1)
                           + dot(low[j][1], u_parts[0], 1, 1))
                out[j, k] = base - product

        @pl.when(p == s)
        def _():
            for k in range(KB):
                out[0, k] = ut[s, k * W:(k + 1) * W, :].T

    store = pltpu.make_async_copy(o_buf, o_hbm, out_sem)
    store.start()
    for copy in sent:
        copy.wait_send()
    for s in range(2):
        @pl.when(p == s)
        def _():
            for t in range(2 * NY):
                if t != s:
                    piece = pl.ds((t % 2) * HALF + (t // 2) * SL, SL)
                    pltpu.make_async_remote_copy(src_ref=tsrc.at[s, piece], dst_ref=tt.at[s, piece],
                                                 send_sem=ts_s.at[s, t], recv_sem=ts_r.at[s], device_id=(t, q),
                                                 device_id_type=MESH).wait_send()
    for n, h in enumerate(HOLDERS):
        @pl.when(q == h)
        def _():
            @pl.loop(1, NQ)
            def _(i):
                piece = pl.ds(0, PR)
                pltpu.make_async_remote_copy(src_ref=loc.at[piece], dst_ref=lp.at[n], send_sem=sc_s.at[i],
                                             recv_sem=sc_r.at[n], device_id=mate, device_id_type=MESH).wait_send()
    store.wait()


def body(matrix, lower_panel, inverses, pivots, panel_owner):
    f32 = jnp.float32
    dma = pltpu.SemaphoreType.DMA
    blocks = matrix.transpose(0, 2, 1, 3)
    any_spec = pl.BlockSpec(memory_space=pl.ANY)
    vmem = pl.BlockSpec(memory_space=pltpu.VMEM)
    line = KB * W
    out = pl.pallas_call(
        kernel,
        out_shape=jax.ShapeDtypeStruct(blocks.shape, f32),
        in_specs=[any_spec, any_spec, vmem, vmem, pl.BlockSpec(memory_space=pltpu.SMEM)],
        out_specs=any_spec,
        scratch_shapes=[
            pltpu.VMEM((2, KB, W, W), f32),
            pltpu.VMEM((2 * W, W), f32),
            pltpu.VMEM((2, line, W), f32),
            pltpu.VMEM((2, HALF, W), f32),
            pltpu.VMEM((2, NY, SL, W), f32),
            pltpu.VMEM((2, 3, SL, W), f32),
            pltpu.VMEM((2, 2, SL, W), f32),
            pltpu.VMEM((2, 4, SL, W), f32),
            pltpu.VMEM((2, line, W), f32),
            pltpu.VMEM((2, line, W), f32),
            pltpu.VMEM((2, line, W), f32),
            pltpu.VMEM((3, PR, W), f32),
            pltpu.VMEM((2, 2 * W, W), f32),
            pltpu.VMEM((2, KB, W, W), f32),
            dma((2,)), dma(()),
            dma((2,)), dma((2,)),
            dma((2, 7)), dma((2, 7)),
            dma((2, 2 * NY)), dma((2,)),
            dma((4, 7)), dma((4, 7)),
            dma((4, 8)), dma((4, 8)),
            dma((NQ,)), dma((3,)),
            dma((NZ,)), dma((NZ,)),
            dma((2, NX)), dma((2, NX)),
        ],
        compiler_params=pltpu.CompilerParams(collective_id=0, has_side_effects=True, vmem_limit_bytes=48 * 2**20),
    )(blocks, lower_panel.reshape(2 * W, W), inverses, pivots, panel_owner)
    return out.transpose(0, 2, 1, 3)


def solution(mesh):
    in_specs = (P(None, "prow", None, "pcol"), P(None, "prow", "pcol"), P(), P(), P())
    return jax.shard_map(body, mesh=mesh, in_specs=in_specs, out_specs=P(None, "prow", None, "pcol"), check_vma=False)
```

```python
import jax
import jax.numpy as jnp
from jax import lax
from jax.experimental import pallas as pl
from jax.experimental.pallas import tpu as pltpu
from jax.sharding import PartitionSpec as P

MESH = pl.DeviceIdType.MESH
W = 256
KB = 3
NY = 8
SL = 48
HALF = NY * SL
NX, NZ = 4, 8
NQ = NX * NZ
PR = 16
HOLDERS = (30, 31, 0)


def split(x):
    hi = x.astype(jnp.bfloat16)
    return hi, (x - hi.astype(jnp.float32)).astype(jnp.bfloat16)


def dot(a, b, ca, cb):
    return lax.dot_general(a, b, (((ca,), (cb,)), ((), ())), preferred_element_type=jnp.float32)


def kernel(a_hbm, l_hbm, inv_hbm, piv_hbm, own_hbm, o_hbm, a, loc, inv_ref, piv_ref, own_ref, pt, pair, s_buf, f_buf, b_buf, r_buf, ut, tt, tsrc,
           lp, lg, o_buf, load_sem, out_sem, pair_s, pair_r, rs_s, rs_r, ts_s, ts_r, ag_s, ag_r, fw_s, fw_r,
           sc_s, sc_r, z_s, z_r, x_s, x_r):
    p, q = lax.axis_index("prow"), lax.axis_index("pcol")
    y, c = p // 2, p % 2
    x, z = q // NZ, q % NZ
    side = 1 - 2 * c

    def at_y(step):
        return (lax.rem(y + step + 2 * NY, NY) * 2 + c, q)

    def chip(step):
        return lax.rem(y + step + 2 * NY, NY)

    mate = (y * 2 + 1 - c, q)

    def at_x(step):
        return (p, lax.rem(x + step, NX) * NZ + z)

    def at_z(step):
        return (p, x * NZ + lax.rem(z + step, NZ))

    sent = []

    def send(src, dst, s, r, to):
        copy = pltpu.make_async_remote_copy(src_ref=src, dst_ref=dst, send_sem=s, recv_sem=r, device_id=to,
                                            device_id_type=MESH)
        copy.start()
        sent.append(copy)
        return copy

    load_a = pltpu.make_async_copy(a_hbm, a, load_sem.at[0])
    load_p = pltpu.make_async_copy(piv_hbm, piv_ref, load_sem.at[1])
    load_rest = [pltpu.make_async_copy(src, dst, load_sem.at[2 + i]) for i, (src, dst) in enumerate(
        ((l_hbm, loc), (inv_hbm, inv_ref), (own_hbm, own_ref)))]
    for copy in [load_p, load_a] + load_rest:
        copy.start()

    barrier = pltpu.get_barrier_semaphore()
    greet = [at_y(i) for i in range(1, NY)] + [mate] + [at_z(i) for i in range(1, NZ)] + [at_x(i) for i in range(1, NX)]
    for to in greet:
        pl.semaphore_signal(barrier, inc=1, device_id=to, device_id_type=MESH)
    for h in HOLDERS:
        @pl.when(q != h)
        def _():
            pl.semaphore_signal(barrier, inc=1, device_id=(p, h), device_id_type=MESH)

    @pl.when(y != 0)
    def _():
        pl.semaphore_signal(barrier, inc=1, device_id=(1 - c, q), device_id_type=MESH)

    def onehot(s, j):
        rows = lax.broadcasted_iota(jnp.int32, (W, W), 0) + (j * 2 * NY + p) * W
        return rows == piv_ref[s:s + 1, :]

    def offer(s):
        hot = [jnp.where(onehot(s, j), 1.0, 0.0).astype(jnp.bfloat16) for j in range(2)]
        for k in range(KB):
            total = jnp.zeros((W, W), jnp.float32)
            for j in range(2):
                for part in split(a[j, k]):
                    total = total + dot(part, hot[j], 0, 0)
            pt[s, k * W:(k + 1) * W, :] = total

    load_p.wait()
    load_a.wait()
    offer(0)

    holds = jnp.logical_or(q == HOLDERS[0], jnp.logical_or(q == HOLDERS[1], q == HOLDERS[2]))
    heard = len(greet) + jnp.where(holds, NQ - 1, 0) + jnp.where(y == 0, NY - 1, 0)
    pl.semaphore_wait(barrier, heard)

    for copy in load_rest:
        copy.wait()
    mine = pl.multiple_of(c * HALF, 8)
    other = pl.multiple_of((1 - c) * HALF, 8)

    def rows_of(step):
        return pl.ds(pl.multiple_of(c * HALF + chip(step) * SL, 8), SL)

    def gather_near(buf, i):
        here = buf.at[rows_of(0)]
        return {st: send(here, here, ag_s.at[i, n], ag_r.at[i, n], at_y(st)) for n, st in enumerate((1, -1, 2, -2))}

    def gather_far(buf, i, near):
        far = []
        near[2].wait_recv()
        from_low = buf.at[rows_of(-2)]
        far.append(send(from_low, from_low, ag_s.at[i, 4], ag_r.at[i, 4], at_y(1)))
        near[-2].wait_recv()
        from_high = buf.at[rows_of(2)]
        far.append(send(from_high, from_high, ag_s.at[i, 5], ag_r.at[i, 5], at_y(-1)))
        across = buf.at[rows_of(-2 * side)]
        far.append(send(across, across, ag_s.at[i, 6], ag_r.at[i, 6], at_y(2 * side)))
        return far

    def share(buf, i, near, far):
        moves = []

        def move(n, step):
            piece = buf.at[rows_of(step)]
            moves.append(send(piece, piece, fw_s.at[i, n], fw_r.at[i, n], mate))

        move(0, 0)
        move(1, 2)
        move(2, -2)
        near[1].wait_recv()
        move(3, -1)
        near[-1].wait_recv()
        move(4, 1)
        far[0].wait_recv()
        move(5, -3)
        far[1].wait_recv()
        move(6, 3)
        far[2].wait_recv()
        move(7, 4)
        return moves

    for s in range(2):
        if s == 1:
            offer(1)
        pair_copy = send(pt.at[s, pl.ds(other, HALF)], pair.at[s], pair_s.at[s], pair_r.at[s], mate)

        @pl.when(p == s)
        def _():
            for k in range(KB):
                tsrc[s, k * W:(k + 1) * W, :] = a[0, k].T
            for t in range(2 * NY):
                piece = pl.ds((t % 2) * HALF + (t // 2) * SL, SL)
                if t == s:
                    tt[s, piece, :] = tsrc[s, piece, :]
                else:
                    pltpu.make_async_remote_copy(src_ref=tsrc.at[s, piece], dst_ref=tt.at[s, piece],
                                                 send_sem=ts_s.at[s, t], recv_sem=ts_r.at[s], device_id=(t, q),
                                                 device_id_type=MESH).start()

        if s == 0:
            for n, h in enumerate(HOLDERS):
                @pl.when(q == h)
                def _():
                    lp[n] = loc[h * PR:(h + 1) * PR, :]

                    @pl.loop(1, NQ)
                    def _(i):
                        to = lax.rem(h + i, NQ)
                        piece = pl.ds(pl.multiple_of(to * PR, 8), PR)
                        pltpu.make_async_remote_copy(src_ref=loc.at[piece], dst_ref=lp.at[n], send_sem=sc_s.at[i],
                                                     recv_sem=sc_r.at[n], device_id=(p, to),
                                                     device_id_type=MESH).start()

        pair_copy.wait_recv()
        for i in range(NY):
            s_buf[s, i] = pt[s, pl.ds(pl.multiple_of(mine + i * SL, 8), SL), :] + pair[s, i * SL:(i + 1) * SL, :]

        far = [
            send(s_buf.at[s, chip(-3)], f_buf.at[s, 0], rs_s.at[s, 0], rs_r.at[s, 0], at_y(-1)),
            send(s_buf.at[s, chip(4)], f_buf.at[s, 1], rs_s.at[s, 1], rs_r.at[s, 1], at_y(-2 * side)),
            send(s_buf.at[s, chip(3)], f_buf.at[s, 2], rs_s.at[s, 2], rs_r.at[s, 2], at_y(1)),
        ]
        near = [
            send(s_buf.at[s, chip(1)], r_buf.at[s, 0], rs_s.at[s, 3], rs_r.at[s, 3], at_y(1)),
            send(s_buf.at[s, chip(-1)], r_buf.at[s, 1], rs_s.at[s, 4], rs_r.at[s, 4], at_y(-1)),
        ]
        for copy in far:
            copy.wait_recv()
        cross = f_buf[s, 1]
        b_buf[s, 0] = s_buf[s, chip(-2)] + f_buf[s, 0] + jnp.where(c == 0, cross, 0.0)
        b_buf[s, 1] = s_buf[s, chip(2)] + f_buf[s, 2] + jnp.where(c == 0, 0.0, cross)
        near += [
            send(b_buf.at[s, 0], r_buf.at[s, 2], rs_s.at[s, 5], rs_r.at[s, 5], at_y(-2)),
            send(b_buf.at[s, 1], r_buf.at[s, 3], rs_s.at[s, 6], rs_r.at[s, 6], at_y(2)),
        ]

        t_here = tt.at[s, rows_of(0)]

        @pl.when(p != s)
        def _():
            pltpu.make_async_remote_copy(src_ref=t_here, dst_ref=t_here, send_sem=ts_s.at[s, 0], recv_sem=ts_r.at[s],
                                         device_id=mate, device_id_type=MESH).wait_recv()
        t_near = gather_near(tt.at[s], 2 * s)

        if s == 0:
            for n, h in enumerate(HOLDERS):
                @pl.when(q != h)
                def _():
                    pltpu.make_async_remote_copy(src_ref=lp.at[n], dst_ref=lp.at[n], send_sem=sc_s.at[0],
                                                 recv_sem=sc_r.at[n], device_id=mate, device_id_type=MESH).wait_recv()
            piece = pl.ds(pl.multiple_of(q * PR, 8), PR)
            for i in range(2):
                chosen = jnp.where(own_ref[i] == HOLDERS[1], lp[1], jnp.where(own_ref[i] == HOLDERS[0], lp[0], lp[2]))
                lg[i, piece, :] = chosen
            z_copies = [send(lg.at[:, piece], lg.at[:, piece], z_s.at[i], z_r.at[i], at_z(i)) for i in range(1, NZ)]

        for copy in near:
            copy.wait_recv()
        total = s_buf[s, y] + r_buf[s, 0] + r_buf[s, 1] + r_buf[s, 2] + r_buf[s, 3]
        ut[s, rows_of(0), :] = lax.dot_general(total, inv_ref[s], (((1,), (1,)), ((), ())),
                                               precision=lax.Precision.HIGHEST, preferred_element_type=jnp.float32)
        u_near = gather_near(ut.at[s], 2 * s + 1)
        t_far = gather_far(tt.at[s], 2 * s, t_near)

        if s == 0:
            for copy in z_copies:
                copy.wait_recv()
            wide = pl.ds(pl.multiple_of(x * (NZ * PR), 8), NZ * PR)
            x_copies = [[send(lg.at[i, wide], lg.at[i, wide], x_s.at[i, n], x_r.at[i, n], at_x(n))
                         for n in range(1, NX)] for i in range(2)]

        u_far = gather_far(ut.at[s], 2 * s + 1, u_near)
        moves = share(tt.at[s], 2 * s, t_near, t_far)
        moves += share(ut.at[s], 2 * s + 1, u_near, u_far)
        for copy in moves:
            copy.wait_recv()
        for copy in x_copies[s]:
            copy.wait_recv()

        hot = [onehot(s, j) for j in range(2)]
        taken = [jnp.sum(jnp.where(h, 1.0, 0.0), axis=1, keepdims=True) > 0.0 for h in hot]
        hot = [jnp.where(h, 1.0, 0.0).astype(jnp.bfloat16) for h in hot]
        low = [jnp.where(p > s, lg[s, :W, :], 0.0), lg[s, W:, :]]
        low = [split(v) for v in low]
        out = a if s == 0 else o_buf
        for k in range(KB):
            cols = pl.ds(k * W, W)
            t_parts = split(tt[s, cols, :])
            u_parts = split(ut[s, cols, :])
            for j in range(2):
                swapped = dot(hot[j], t_parts[0], 1, 1) + dot(hot[j], t_parts[1], 1, 1)
                base = jnp.where(taken[j], swapped, a[j, k])
                product = (dot(low[j][0], u_parts[0], 1, 1) + dot(low[j][0], u_parts[1], 1, 1)
                           + dot(low[j][1], u_parts[0], 1, 1))
                out[j, k] = base - product

        @pl.when(p == s)
        def _():
            for k in range(KB):
                out[0, k] = ut[s, k * W:(k + 1) * W, :].T

    store = pltpu.make_async_copy(o_buf, o_hbm, out_sem)
    store.start()
    for copy in sent:
        copy.wait_send()
    for s in range(2):
        @pl.when(p == s)
        def _():
            for t in range(2 * NY):
                if t != s:
                    piece = pl.ds((t % 2) * HALF + (t // 2) * SL, SL)
                    pltpu.make_async_remote_copy(src_ref=tsrc.at[s, piece], dst_ref=tt.at[s, piece],
                                                 send_sem=ts_s.at[s, t], recv_sem=ts_r.at[s], device_id=(t, q),
                                                 device_id_type=MESH).wait_send()
    for n, h in enumerate(HOLDERS):
        @pl.when(q == h)
        def _():
            @pl.loop(1, NQ)
            def _(i):
                piece = pl.ds(0, PR)
                pltpu.make_async_remote_copy(src_ref=loc.at[piece], dst_ref=lp.at[n], send_sem=sc_s.at[i],
                                             recv_sem=sc_r.at[n], device_id=mate, device_id_type=MESH).wait_send()
    store.wait()


def body(matrix, lower_panel, inverses, pivots, panel_owner):
    f32 = jnp.float32
    dma = pltpu.SemaphoreType.DMA
    blocks = matrix.transpose(0, 2, 1, 3)
    any_spec = pl.BlockSpec(memory_space=pl.ANY)
    line = KB * W
    out = pl.pallas_call(
        kernel,
        out_shape=jax.ShapeDtypeStruct(blocks.shape, f32),
        in_specs=[any_spec] * 5,
        out_specs=any_spec,
        scratch_shapes=[
            pltpu.VMEM((2, KB, W, W), f32),
            pltpu.VMEM((2 * W, W), f32),
            pltpu.VMEM((2, W, W), f32),
            pltpu.VMEM((2, W), jnp.int32),
            pltpu.SMEM((2,), jnp.int32),
            pltpu.VMEM((2, line, W), f32),
            pltpu.VMEM((2, HALF, W), f32),
            pltpu.VMEM((2, NY, SL, W), f32),
            pltpu.VMEM((2, 3, SL, W), f32),
            pltpu.VMEM((2, 2, SL, W), f32),
            pltpu.VMEM((2, 4, SL, W), f32),
            pltpu.VMEM((2, line, W), f32),
            pltpu.VMEM((2, line, W), f32),
            pltpu.VMEM((2, line, W), f32),
            pltpu.VMEM((3, PR, W), f32),
            pltpu.VMEM((2, 2 * W, W), f32),
            pltpu.VMEM((2, KB, W, W), f32),
            dma((5,)), dma(()),
            dma((2,)), dma((2,)),
            dma((2, 7)), dma((2, 7)),
            dma((2, 2 * NY)), dma((2,)),
            dma((4, 7)), dma((4, 7)),
            dma((4, 8)), dma((4, 8)),
            dma((NQ,)), dma((3,)),
            dma((NZ,)), dma((NZ,)),
            dma((2, NX)), dma((2, NX)),
        ],
        compiler_params=pltpu.CompilerParams(collective_id=0, has_side_effects=True, vmem_limit_bytes=60 * 2**20),
    )(blocks, lower_panel.reshape(2 * W, W), inverses, pivots, panel_owner)
    return out.transpose(0, 2, 1, 3)


def solution(mesh):
    in_specs = (P(None, "prow", None, "pcol"), P(None, "prow", "pcol"), P(), P(), P())
    return jax.shard_map(body, mesh=mesh, in_specs=in_specs, out_specs=P(None, "prow", None, "pcol"), check_vma=False)
```

```python
import jax
import jax.numpy as jnp
from jax import lax
from jax.experimental import pallas as pl
from jax.experimental.pallas import tpu as pltpu
from jax.sharding import PartitionSpec as P

MESH = pl.DeviceIdType.MESH
W = 256
KB = 3
NY = 8
ST = 2
SL = 24
WIDE = 2 * NY * SL
NX, NZ = 4, 8
NQ = NX * NZ
PR = 16
HOLDERS = (30, 31, 0)


def split(x):
    hi = x.astype(jnp.bfloat16)
    return hi, (x - hi.astype(jnp.float32)).astype(jnp.bfloat16)


def dot(a, b, ca, cb):
    return lax.dot_general(a, b, (((ca,), (cb,)), ((), ())), preferred_element_type=jnp.float32)


def dot3(a, b):
    return dot(a[0], b[0], 1, 1) + dot(a[0], b[1], 1, 1) + dot(a[1], b[0], 1, 1)


def as_hot(mask):
    return jnp.where(mask, 1.0, 0.0).astype(jnp.bfloat16)


def kernel(a_hbm, l_hbm, inv_hbm, piv_hbm, own_hbm, o_hbm, a, loc, inv_ref, piv_ref, own_ref, pt, pair, s_buf, f_buf,
           b_buf, g_buf, d_buf, r_buf, ut, tt, tsrc, lp, lg, et, ep, es, er, ms, mr, mn, t1, u1, o_buf, load_sem, out_sem, pair_s,
           pair_r, rs_s, rs_r, ts_s, ts_r, ag_s, ag_r, fw_s, fw_r, sc_s, sc_r, z_s, z_r, x_s, x_r, e_s, e_r, n_s, n_r,
           m_s, m_r):
    p, q = lax.axis_index("prow"), lax.axis_index("pcol")
    y, c = p // 2, p % 2
    x, z = q // NZ, q % NZ
    side = 1 - 2 * c

    def chip(step):
        return lax.rem(y + step + 2 * NY, NY)

    def at_y(step):
        return (chip(step) * 2 + c, q)

    mate = (y * 2 + 1 - c, q)

    def at_x(step):
        return (p, lax.rem(x + step, NX) * NZ + z)

    def at_z(step):
        return (p, x * NZ + lax.rem(z + step, NZ))

    sent = []

    def remote(src, dst, s, r, to):
        return pltpu.make_async_remote_copy(src_ref=src, dst_ref=dst, send_sem=s, recv_sem=r, device_id=to,
                                            device_id_type=MESH)

    def send(src, dst, s, r, to):
        copy = remote(src, dst, s, r, to)
        copy.start()
        sent.append(copy)
        return copy

    def settle(copies):
        for copy in copies:
            copy.wait_recv()

    load_a = pltpu.make_async_copy(a_hbm, a, load_sem.at[0])
    load_p = pltpu.make_async_copy(piv_hbm, piv_ref, load_sem.at[1])
    load_rest = [pltpu.make_async_copy(src, dst, load_sem.at[2 + i]) for i, (src, dst) in enumerate(
        ((l_hbm, loc), (inv_hbm, inv_ref), (own_hbm, own_ref)))]
    for copy in [load_p, load_a] + load_rest:
        copy.start()

    barrier = pltpu.get_barrier_semaphore()
    for h in HOLDERS:
        @pl.when(q != h)
        def _():
            pl.semaphore_signal(barrier, inc=1, device_id=(p, h), device_id_type=MESH)
    greet = [at_y(i) for i in range(1, NY)] + [mate] + [at_z(i) for i in range(1, NZ)] + [at_x(i) for i in range(1, NX)]
    for to in greet:
        pl.semaphore_signal(barrier, inc=1, device_id=to, device_id_type=MESH)

    @pl.when(y != 0)
    def _():
        pl.semaphore_signal(barrier, inc=1, device_id=(1 - c, q), device_id_type=MESH)

    def onehot(j, wanted):
        rows = lax.broadcasted_iota(jnp.int32, (W, W), 0) + (j * 2 * NY + p) * W
        return rows == wanted

    def pick(wanted):
        hot = [as_hot(onehot(j, wanted)) for j in range(2)]
        blocks = []
        for k in range(KB):
            total = jnp.zeros((W, W), jnp.float32)
            for j in range(2):
                for part in split(a[j, k]):
                    total = total + dot(part, hot[j], 0, 0)
            blocks.append(total)
        return jnp.concatenate(blocks, axis=0).reshape(ST, 2, NY, SL, W)

    load_p.wait()
    load_a.wait()
    pt[0] = pick(piv_ref[0:1, :])

    holds = jnp.logical_or(q == HOLDERS[0], jnp.logical_or(q == HOLDERS[1], q == HOLDERS[2]))
    heard = len(greet) + jnp.where(holds, NQ - 1, 0) + jnp.where(y == 0, NY - 1, 0)
    pl.semaphore_wait(barrier, heard)

    for copy in load_rest:
        copy.wait()

    def scatter(n):
        h = HOLDERS[n]

        @pl.when(q == h)
        def _():
            lp[n] = loc[h * PR:(h + 1) * PR, :]

            @pl.loop(1, NQ)
            def _(i):
                to = lax.rem(h + i, NQ)
                piece = pl.ds(pl.multiple_of(to * PR, 8), PR)
                pltpu.make_async_remote_copy(src_ref=loc.at[piece], dst_ref=lp.at[n], send_sem=sc_s.at[i],
                                             recv_sem=sc_r.at[n], device_id=(p, to), device_id_type=MESH).start()

    def arrived(n):
        @pl.when(q != HOLDERS[n])
        def _():
            pltpu.make_async_remote_copy(src_ref=lp.at[n], dst_ref=lp.at[n], send_sem=sc_s.at[0],
                                         recv_sem=sc_r.at[n], device_id=mate, device_id_type=MESH).wait_recv()

    l_rows = pl.ds(pl.multiple_of(q * PR, 8), PR)
    l_wide = pl.ds(pl.multiple_of(x * (NZ * PR), 8), NZ * PR)

    def gather_z(i):
        lg[i, l_rows, :] = jnp.where(own_ref[i] == HOLDERS[1], lp[1], lp[2 * i])
        piece = lg.at[i, l_rows]
        return [send(piece, piece, z_s.at[i, n], z_r.at[i, n], at_z(n)) for n in range(1, NZ)]

    def gather_x(i):
        piece = lg.at[i, l_wide]
        return [send(piece, piece, x_s.at[i, n], x_r.at[i, n], at_x(n)) for n in range(1, NX)]

    def pair_up(s, h):
        return send(pt.at[s, h, 1 - c], pair.at[s, h], pair_s.at[s, h], pair_r.at[s, h], mate)

    def reduce_first(s, h, pair_copy):
        pair_copy.wait_recv()
        s_buf[s, h] = pt[s, h, c] + pair[s, h]
        plan = ((-3, -1), (4, -2 * side), (3, 1))
        return [send(s_buf.at[s, h, chip(end)], f_buf.at[s, h, n], rs_s.at[s, h, n], rs_r.at[s, h, n], at_y(to))
                for n, (end, to) in enumerate(plan)]

    def reduce_second(s, h, first):
        settle(first)
        cross = f_buf[s, h, 1]
        b_buf[s, h, 0] = s_buf[s, h, chip(-2)] + f_buf[s, h, 0] + jnp.where(c == 0, cross, 0.0)
        b_buf[s, h, 1] = s_buf[s, h, chip(2)] + f_buf[s, h, 2] + jnp.where(c == 0, 0.0, cross)
        return [send(b_buf.at[s, h, n], g_buf.at[s, h, n], rs_s.at[s, h, 3 + n], rs_r.at[s, h, 3 + n], at_y(to))
                for n, to in enumerate((-1, 1))]

    def reduce_third(s, h, second):
        settle(second)
        d_buf[s, h, 0] = s_buf[s, h, chip(-1)] + g_buf[s, h, 0]
        d_buf[s, h, 1] = s_buf[s, h, chip(1)] + g_buf[s, h, 1]
        return [send(d_buf.at[s, h, n], r_buf.at[s, h, n], rs_s.at[s, h, 5 + n], rs_r.at[s, h, 5 + n], at_y(to))
                for n, to in enumerate((-1, 1))]

    def solve(s, h, last):
        settle(last)
        total = s_buf[s, h, y] + r_buf[s, h, 0] + r_buf[s, h, 1]
        ut[s, h, c, y] = lax.dot_general(total, inv_ref[s], (((1,), (1,)), ((), ())),
                                         precision=lax.Precision.HIGHEST, preferred_element_type=jnp.float32)

    def upper_piece(s, h):
        return lambda step: ut.at[s, h, c, chip(step)]

    def top_piece(s):
        return lambda step: tt.at[s, :, c, chip(step)]

    def gather_first(piece, i):
        return [send(piece(0), piece(0), ag_s.at[i, n], ag_r.at[i, n], at_y(to)) for n, to in enumerate((1, -1))]

    def gather_second(piece, i, first):
        copies = []
        for n, to in enumerate((1, -1)):
            first[n].wait_recv()
            copies.append(send(piece(-to), piece(-to), ag_s.at[i, 2 + n], ag_r.at[i, 2 + n], at_y(to)))
        return copies

    def gather_third(piece, i, second):
        copies = []
        for n, to in enumerate((1, -1)):
            second[n].wait_recv()
            copies.append(send(piece(-2 * to), piece(-2 * to), ag_s.at[i, 4 + n], ag_r.at[i, 4 + n], at_y(to)))
        over = piece(-2 * side)
        return copies + [send(over, over, ag_s.at[i, 6], ag_r.at[i, 6], at_y(2 * side))]

    def share(half, i, far):
        settle(far)
        return send(half, half, fw_s.at[i], fw_r.at[i], mate)

    def spread_top(s):
        @pl.when(p == s)
        def _():
            tsrc[s] = jnp.concatenate([a[0, k].T for k in range(KB)], axis=0).reshape(ST, 2, NY, SL, W)
            for t in range(2 * NY):
                src, dst = tsrc.at[s, :, t % 2, t // 2], tt.at[s, :, t % 2, t // 2]
                if t == s:
                    tt[s, :, t % 2, t // 2] = tsrc[s, :, t % 2, t // 2]
                else:
                    pltpu.make_async_remote_copy(src_ref=src, dst_ref=dst, send_sem=ts_s.at[s, t], recv_sem=ts_r.at[s],
                                                 device_id=(t, q), device_id_type=MESH).start()

    def gather_top(s):
        here = tt.at[s, :, c, y]

        @pl.when(p != s)
        def _():
            pltpu.make_async_remote_copy(src_ref=here, dst_ref=here, send_sem=ts_s.at[s, 0], recv_sem=ts_r.at[s],
                                         device_id=mate, device_id_type=MESH).wait_recv()
        return gather_first(top_piece(s), 3 * s + 2)

    def swap(s, j, tops):
        mask = onehot(j, piv_ref[s:s + 1, :])
        taken = jnp.sum(jnp.where(mask, 1.0, 0.0), axis=1, keepdims=True) > 0.0
        hot = as_hot(mask)
        new = []
        for k in range(KB):
            hi, lo = split(tops[k * W:(k + 1) * W])
            new.append(jnp.where(taken, dot(hot, hi, 1, 1) + dot(hot, lo, 1, 1), a[j, k]))
        return new

    def below(s, j):
        return split(lg[s, W:, :] if j else jnp.where(p > s, lg[s, :W, :], 0.0))

    def update(j):
        new = swap(0, j, tt[0].reshape(KB * W, W))
        low = below(0, j)
        upper = ut[0].reshape(KB * W, W)
        for k in range(KB):
            a[j, k] = new[k] - dot3(low, split(upper[k * W:(k + 1) * W]))

    lined = jnp.logical_or(q == HOLDERS[0], q == HOLDERS[1])

    def rows_first():
        @pl.when(lined)
        def _():
            hot = [as_hot(onehot(j, piv_ref[1:2, :])) for j in range(2)]
            total = jnp.zeros((W, W), jnp.float32)
            for j in range(2):
                for part in split(loc[j * W:(j + 1) * W, :]):
                    total = total + dot(hot[j], part, 0, 0)
            et[...] = total.reshape(2, NY, PR, W)
            remote(et.at[1 - c], ep, e_s.at[0], e_r.at[0], mate).start()

            @pl.when(p == 1)
            def _():
                for t in range(2 * NY):
                    piece = pl.ds((t % 2) * NY * PR + (t // 2) * PR, PR)
                    if t == 1:
                        ms[1] = loc[piece, :]
                    else:
                        remote(loc.at[piece], ms.at[1], n_s.at[t], n_r, (t, q)).start()

    def rows_second():
        @pl.when(lined)
        def _():
            remote(et.at[1 - c], ep, e_s.at[0], e_r.at[0], mate).wait_recv()
            es[...] = et[c] + ep[...]
            for i in range(1, NY):
                remote(es.at[chip(i)], er.at[i - 1], e_s.at[i], e_r.at[i], at_y(i)).start()

    def rows_third():
        @pl.when(lined)
        def _():
            total = es[y]
            for i in range(1, NY):
                remote(es.at[chip(i)], er.at[i - 1], e_s.at[i], e_r.at[i], at_y(i)).wait_recv()
                total = total + er[i - 1]
            ms[0] = total

            @pl.when(p != 1)
            def _():
                remote(ms.at[1], ms.at[1], n_s.at[0], n_r, mate).wait_recv()
        for n in range(2):
            @pl.when(q == HOLDERS[n])
            def _():
                mr[n] = ms[...]
                for i in range(1, NX):
                    remote(mr.at[n], mr.at[n], m_s.at[i], m_r.at[n], at_x(i)).start()

    def rows_fourth():
        for n in range(2):
            @pl.when(z == HOLDERS[n] % NZ)
            def _():
                @pl.when(q != HOLDERS[n])
                def _():
                    remote(mr.at[n], mr.at[n], m_s.at[0], m_r.at[n], mate).wait_recv()
                for i in range(1, NZ):
                    remote(mr.at[n], mr.at[n], m_s.at[NX + i], m_r.at[n], at_z(i)).start()

    def rows_here():
        for n in range(2):
            @pl.when(z != HOLDERS[n] % NZ)
            def _():
                remote(mr.at[n], mr.at[n], m_s.at[0], m_r.at[n], mate).wait_recv()
        mn[:, c, y] = jnp.where(own_ref[0] == HOLDERS[0], mr[0], mr[1])

    def rows_piece(step):
        return mn.at[:, c, chip(step)]

    every = [(s, h) for s in range(2) for h in range(ST)]
    slot = {(s, h): 3 * s + h for s, h in every}

    pairs = {(0, h): pair_up(0, h) for h in range(ST)}
    rows_first()

    first = jnp.broadcast_to(piv_ref[0:1, :].astype(jnp.float32), (W, W)).T
    hit = jnp.where(first == piv_ref[1:2, :].astype(jnp.float32), 1.0, 0.0)
    place = jnp.sum(hit * lax.broadcasted_iota(jnp.int32, (W, W), 0).astype(jnp.float32), axis=0, keepdims=True)
    moved = jnp.sum(hit, axis=0, keepdims=True) > 0.0
    pt[1] = pick(jnp.where(moved, place.astype(jnp.int32), piv_ref[1:2, :]))
    pairs.update({(1, h): pair_up(1, h) for h in range(ST)})

    work = {k: reduce_first(*k, pairs[k]) for k in every}
    rows_second()
    for n in range(len(HOLDERS)):
        scatter(n)
    for s in range(2):
        spread_top(s)
    work = {k: reduce_second(*k, work[k]) for k in every}
    rows_third()
    for n in range(len(HOLDERS)):
        arrived(n)
    z_copies = [gather_z(i) for i in range(2)]
    work = {k: reduce_third(*k, work[k]) for k in every}
    rows_fourth()
    upper = {}
    for k in every:
        solve(*k, work[k])
        upper[k] = gather_first(upper_piece(*k), slot[k])
    tops = [gather_top(s) for s in range(2)]
    x_copies = []
    for i in range(2):
        settle(z_copies[i])
        x_copies.append(gather_x(i))
    upper = {k: gather_second(upper_piece(*k), slot[k], upper[k]) for k in every}
    tops = [gather_second(top_piece(s), 3 * s + 2, tops[s]) for s in range(2)]
    rows_here()
    rows = gather_first(rows_piece, 6)
    upper = {k: gather_third(upper_piece(*k), slot[k], upper[k]) for k in every}
    tops = [gather_third(top_piece(s), 3 * s + 2, tops[s]) for s in range(2)]
    rows = gather_second(rows_piece, 6, rows)
    upper = {k: share(ut.at[k[0], k[1], c], slot[k], upper[k]) for k in every}
    rows = gather_third(rows_piece, 6, rows)
    tops = [share(tt.at[s, :, c], 3 * s + 2, tops[s]) for s in range(2)]
    rows = share(mn.at[:, c], 6, rows)

    settle(tops)
    settle(x_copies[0])
    for h in range(ST):
        upper[0, h].wait_recv()
    for j in range(2):
        update(j)

    @pl.when(p == 0)
    def _():
        whole = ut[0].reshape(KB * W, W)
        for k in range(KB):
            a[0, k] = whole[k * W:(k + 1) * W].T

    rows.wait_recv()
    solved = [split(ut[0, h].reshape(WIDE, W)) for h in range(ST)]
    ids = lax.broadcasted_iota(jnp.int32, (W, W), 1) + W
    link = first == ids.astype(jnp.float32)
    linked = jnp.sum(jnp.where(link, 1.0, 0.0), axis=0, keepdims=True) > 0.0
    link = as_hot(link)
    second = split(mn[1].reshape(W, W))
    for h in range(ST):
        hi, lo = split(tt[0, h].reshape(WIDE, W))
        raw = jnp.where(linked, dot(hi, link, 1, 0) + dot(lo, link, 1, 0), tt[1, h].reshape(WIDE, W))
        t1[h * WIDE:(h + 1) * WIDE, :] = raw - dot3(solved[h], second)
    for j in range(2):
        for k, block in enumerate(swap(1, j, t1[...])):
            o_buf[j, k] = block
    mixed = split(lax.dot_general(inv_ref[1], mn[0].reshape(W, W), (((1,), (0,)), ((), ())),
                                  precision=lax.Precision.HIGHEST, preferred_element_type=jnp.float32))
    drop = [dot3(solved[h], mixed) for h in range(ST)]
    settle(x_copies[1])
    low = [below(1, j) for j in range(2)]
    for h in range(ST):
        upper[1, h].wait_recv()
        solved1 = ut[1, h].reshape(WIDE, W) - drop[h]
        u1[h * WIDE:(h + 1) * WIDE, :] = solved1
        solved1 = split(solved1)
        for j in range(2):
            product = dot3(low[j], solved1)
            at = h * (W // 2)
            part = pl.ds(at, W // 2)
            o_buf[j, 2 * h] = o_buf[j, 2 * h] - product[:, at:at + W]
            rest = product[:, :W // 2] if h else product[:, W:]
            o_buf[j, 1, :, part] = o_buf[j, 1, :, part] - rest

    @pl.when(p == 1)
    def _():
        for k in range(KB):
            o_buf[0, k] = u1[k * W:(k + 1) * W, :].T

    store = pltpu.make_async_copy(o_buf, o_hbm, out_sem)
    store.start()
    for copy in sent:
        copy.wait_send()
    for s in range(2):
        @pl.when(p == s)
        def _():
            for t in range(2 * NY):
                if t != s:
                    piece = tsrc.at[s, :, t % 2, t // 2]
                    pltpu.make_async_remote_copy(src_ref=piece, dst_ref=piece, send_sem=ts_s.at[s, t],
                                                 recv_sem=ts_r.at[s], device_id=mate, device_id_type=MESH).wait_send()
    for n, h in enumerate(HOLDERS):
        @pl.when(q == h)
        def _():
            @pl.loop(1, NQ)
            def _(i):
                piece = loc.at[pl.ds(0, PR)]
                pltpu.make_async_remote_copy(src_ref=piece, dst_ref=piece, send_sem=sc_s.at[i], recv_sem=sc_r.at[n],
                                             device_id=mate, device_id_type=MESH).wait_send()

    @pl.when(lined)
    def _():
        remote(et.at[1 - c], ep, e_s.at[0], e_r.at[0], mate).wait_send()
        for i in range(1, NY):
            remote(es.at[chip(i)], er.at[i - 1], e_s.at[i], e_r.at[i], at_y(i)).wait_send()

        @pl.when(p == 1)
        def _():
            for t in range(2 * NY):
                if t != 1:
                    remote(loc.at[pl.ds(0, PR)], ms.at[1], n_s.at[t], n_r, mate).wait_send()

    for n in range(2):
        @pl.when(q == HOLDERS[n])
        def _():
            for i in range(1, NX):
                remote(mr.at[n], mr.at[n], m_s.at[i], m_r.at[n], mate).wait_send()

        @pl.when(z == HOLDERS[n] % NZ)
        def _():
            for i in range(1, NZ):
                remote(mr.at[n], mr.at[n], m_s.at[NX + i], m_r.at[n], mate).wait_send()
    store.wait()


def body(matrix, lower_panel, inverses, pivots, panel_owner):
    f32 = jnp.float32
    dma = pltpu.SemaphoreType.DMA
    blocks = matrix.transpose(0, 2, 1, 3)
    any_spec = pl.BlockSpec(memory_space=pl.ANY)
    line = (ST, 2, NY, SL, W)
    out = pl.pallas_call(
        kernel,
        out_shape=jax.ShapeDtypeStruct(blocks.shape, f32),
        in_specs=[any_spec] * 5,
        out_specs=any_spec,
        scratch_shapes=[
            pltpu.VMEM((2, KB, W, W), f32),
            pltpu.VMEM((2 * W, W), f32),
            pltpu.VMEM((2, W, W), f32),
            pltpu.VMEM((2, W), jnp.int32),
            pltpu.SMEM((2,), jnp.int32),
            pltpu.VMEM((2,) + line, f32),
            pltpu.VMEM((2, ST, NY, SL, W), f32),
            pltpu.VMEM((2, ST, NY, SL, W), f32),
            pltpu.VMEM((2, ST, 3, SL, W), f32),
            pltpu.VMEM((2, ST, 2, SL, W), f32),
            pltpu.VMEM((2, ST, 2, SL, W), f32),
            pltpu.VMEM((2, ST, 2, SL, W), f32),
            pltpu.VMEM((2, ST, 2, SL, W), f32),
            pltpu.VMEM((2,) + line, f32),
            pltpu.VMEM((2,) + line, f32),
            pltpu.VMEM((2,) + line, f32),
            pltpu.VMEM((3, PR, W), f32),
            pltpu.VMEM((2, 2 * W, W), f32),
            pltpu.VMEM((2, NY, PR, W), f32),
            pltpu.VMEM((NY, PR, W), f32),
            pltpu.VMEM((NY, PR, W), f32),
            pltpu.VMEM((NY - 1, PR, W), f32),
            pltpu.VMEM((2, PR, W), f32),
            pltpu.VMEM((2, 2, PR, W), f32),
            pltpu.VMEM((2, 2, NY, PR, W), f32),
            pltpu.VMEM((KB * W, W), f32),
            pltpu.VMEM((KB * W, W), f32),
            pltpu.VMEM((2, KB, W, W), f32),
            dma((5,)), dma(()),
            dma((2, ST)), dma((2, ST)),
            dma((2, ST, 7)), dma((2, ST, 7)),
            dma((2, 2 * NY)), dma((2,)),
            dma((7, 7)), dma((7, 7)),
            dma((7,)), dma((7,)),
            dma((NQ,)), dma((3,)),
            dma((2, NZ)), dma((2, NZ)),
            dma((2, NX)), dma((2, NX)),
            dma((NY,)), dma((NY,)),
            dma((2 * NY,)), dma(()),
            dma((NX + NZ,)), dma((2,)),
        ],
        compiler_params=pltpu.CompilerParams(collective_id=0, has_side_effects=True, vmem_limit_bytes=60 * 2**20),
    )(blocks, lower_panel.reshape(2 * W, W), inverses, pivots, panel_owner)
    return out.transpose(0, 2, 1, 3)


def solution(mesh):
    in_specs = (P(None, "prow", None, "pcol"), P(None, "prow", "pcol"), P(), P(), P())
    return jax.shard_map(body, mesh=mesh, in_specs=in_specs, out_specs=P(None, "prow", None, "pcol"), check_vma=False)
```

```python
import jax
import jax.numpy as jnp
from jax import lax
from jax.experimental import pallas as pl
from jax.experimental.pallas import tpu as pltpu
from jax.sharding import PartitionSpec as P

MESH = pl.DeviceIdType.MESH
W = 256
KB = 3
NY = 8
ST = 2
SL = 24
WIDE = 2 * NY * SL
NX, NZ = 4, 8
NQ = NX * NZ
PR = 16
HOLDERS = (30, 31, 0)


def split(x):
    hi = x.astype(jnp.bfloat16)
    return hi, (x - hi.astype(jnp.float32)).astype(jnp.bfloat16)


def dot(a, b, ca, cb):
    return lax.dot_general(a, b, (((ca,), (cb,)), ((), ())), preferred_element_type=jnp.float32)


def dot3(a, b):
    return dot(a[0], b[0], 1, 1) + dot(a[0], b[1], 1, 1) + dot(a[1], b[0], 1, 1)


def as_hot(mask):
    return jnp.where(mask, 1.0, 0.0).astype(jnp.bfloat16)


def kernel(a_hbm, l_hbm, inv_hbm, piv_hbm, own_hbm, o_hbm, a, loc, inv_ref, piv_ref, own_ref, pt, pair, s_buf, f_buf,
           b_buf, g_buf, d_buf, r_buf, ut, tt, tsrc, lp, lg, et, ep, es, er, ms, mr, mn, t1, u1, o_buf, load_sem, out_sem, pair_s,
           pair_r, rs_s, rs_r, ts_s, ts_r, ag_s, ag_r, fw_s, fw_r, sc_s, sc_r, z_s, z_r, x_s, x_r, e_s, e_r, n_s, n_r,
           m_s, m_r):
    p, q = lax.axis_index("prow"), lax.axis_index("pcol")
    y, c = p // 2, p % 2
    x, z = q // NZ, q % NZ
    side = 1 - 2 * c

    def chip(step):
        return lax.rem(y + step + 2 * NY, NY)

    def at_y(step):
        return (chip(step) * 2 + c, q)

    mate = (y * 2 + 1 - c, q)

    def at_x(step):
        return (p, lax.rem(x + step, NX) * NZ + z)

    def at_z(step):
        return (p, x * NZ + lax.rem(z + step, NZ))

    sent = []

    def remote(src, dst, s, r, to):
        return pltpu.make_async_remote_copy(src_ref=src, dst_ref=dst, send_sem=s, recv_sem=r, device_id=to,
                                            device_id_type=MESH)

    def send(src, dst, s, r, to):
        copy = remote(src, dst, s, r, to)
        copy.start()
        sent.append(copy)
        return copy

    def settle(copies):
        for copy in copies:
            copy.wait_recv()

    load_a = pltpu.make_async_copy(a_hbm, a, load_sem.at[0])
    load_p = pltpu.make_async_copy(piv_hbm, piv_ref, load_sem.at[1])
    load_rest = [pltpu.make_async_copy(src, dst, load_sem.at[2 + i]) for i, (src, dst) in enumerate(
        ((l_hbm, loc), (inv_hbm, inv_ref), (own_hbm, own_ref)))]
    for copy in [load_p, load_a] + load_rest:
        copy.start()

    barrier = pltpu.get_barrier_semaphore()
    for h in HOLDERS:
        @pl.when(q != h)
        def _():
            pl.semaphore_signal(barrier, inc=1, device_id=(p, h), device_id_type=MESH)
    greet = [at_y(i) for i in range(1, NY)] + [mate] + [at_z(i) for i in range(1, NZ)] + [at_x(i) for i in range(1, NX)]
    for to in greet:
        pl.semaphore_signal(barrier, inc=1, device_id=to, device_id_type=MESH)

    @pl.when(y != 0)
    def _():
        pl.semaphore_signal(barrier, inc=1, device_id=(1 - c, q), device_id_type=MESH)

    def onehot(j, wanted):
        rows = lax.broadcasted_iota(jnp.int32, (W, W), 0) + (j * 2 * NY + p) * W
        return rows == wanted

    def pick(wanted):
        hot = [as_hot(onehot(j, wanted)) for j in range(2)]
        blocks = []
        for k in range(KB):
            total = jnp.zeros((W, W), jnp.float32)
            for j in range(2):
                for part in split(a[j, k]):
                    total = total + dot(part, hot[j], 0, 0)
            blocks.append(total)
        return jnp.concatenate(blocks, axis=0).reshape(ST, 2, NY, SL, W)

    load_p.wait()
    load_a.wait()
    pt[0] = pick(piv_ref[0:1, :])

    holds = jnp.logical_or(q == HOLDERS[0], jnp.logical_or(q == HOLDERS[1], q == HOLDERS[2]))
    heard = len(greet) + jnp.where(holds, NQ - 1, 0) + jnp.where(y == 0, NY - 1, 0)
    pl.semaphore_wait(barrier, heard)

    for copy in load_rest:
        copy.wait()

    def scatter(n):
        h = HOLDERS[n]

        @pl.when(q == h)
        def _():
            lp[n] = loc[h * PR:(h + 1) * PR, :]

            @pl.loop(1, NQ)
            def _(i):
                to = lax.rem(h + i, NQ)
                piece = pl.ds(pl.multiple_of(to * PR, 8), PR)
                pltpu.make_async_remote_copy(src_ref=loc.at[piece], dst_ref=lp.at[n], send_sem=sc_s.at[i],
                                             recv_sem=sc_r.at[n], device_id=(p, to), device_id_type=MESH).start()

    def arrived(n):
        @pl.when(q != HOLDERS[n])
        def _():
            pltpu.make_async_remote_copy(src_ref=lp.at[n], dst_ref=lp.at[n], send_sem=sc_s.at[0],
                                         recv_sem=sc_r.at[n], device_id=mate, device_id_type=MESH).wait_recv()

    l_rows = pl.ds(pl.multiple_of(q * PR, 8), PR)
    l_wide = pl.ds(pl.multiple_of(x * (NZ * PR), 8), NZ * PR)

    def gather_z(i):
        lg[i, l_rows, :] = jnp.where(own_ref[i] == HOLDERS[1], lp[1], lp[2 * i])
        piece = lg.at[i, l_rows]
        return [send(piece, piece, z_s.at[i, n], z_r.at[i, n], at_z(n)) for n in range(1, NZ)]

    def gather_x(i):
        piece = lg.at[i, l_wide]
        return [send(piece, piece, x_s.at[i, n], x_r.at[i, n], at_x(n)) for n in range(1, NX)]

    def pair_up(s, h):
        return send(pt.at[s, h, 1 - c], pair.at[s, h], pair_s.at[s, h], pair_r.at[s, h], mate)

    def reduce_first(s, h, pair_copy):
        pair_copy.wait_recv()
        s_buf[s, h] = pt[s, h, c] + pair[s, h]
        plan = ((-3, -1), (4, -2 * side), (3, 1))
        return [send(s_buf.at[s, h, chip(end)], f_buf.at[s, h, n], rs_s.at[s, h, n], rs_r.at[s, h, n], at_y(to))
                for n, (end, to) in enumerate(plan)]

    def reduce_second(s, h, first):
        settle(first)
        cross = f_buf[s, h, 1]
        b_buf[s, h, 0] = s_buf[s, h, chip(-2)] + f_buf[s, h, 0] + jnp.where(c == 0, cross, 0.0)
        b_buf[s, h, 1] = s_buf[s, h, chip(2)] + f_buf[s, h, 2] + jnp.where(c == 0, 0.0, cross)
        return [send(b_buf.at[s, h, n], g_buf.at[s, h, n], rs_s.at[s, h, 3 + n], rs_r.at[s, h, 3 + n], at_y(to))
                for n, to in enumerate((-1, 1))]

    def reduce_third(s, h, second):
        settle(second)
        d_buf[s, h, 0] = s_buf[s, h, chip(-1)] + g_buf[s, h, 0]
        d_buf[s, h, 1] = s_buf[s, h, chip(1)] + g_buf[s, h, 1]
        return [send(d_buf.at[s, h, n], r_buf.at[s, h, n], rs_s.at[s, h, 5 + n], rs_r.at[s, h, 5 + n], at_y(to))
                for n, to in enumerate((-1, 1))]

    def solve(s, h, last):
        settle(last)
        total = s_buf[s, h, y] + r_buf[s, h, 0] + r_buf[s, h, 1]
        ut[s, h, c, y] = lax.dot_general(total, inv_ref[s], (((1,), (1,)), ((), ())),
                                         precision=lax.Precision.HIGHEST, preferred_element_type=jnp.float32)

    def upper_piece(s, h):
        return lambda step: ut.at[s, h, c, chip(step)]

    def top_piece(s):
        return lambda step: tt.at[s, :, c, chip(step)]

    def gather_first(piece, i):
        return [send(piece(0), piece(0), ag_s.at[i, n], ag_r.at[i, n], at_y(to)) for n, to in enumerate((1, -1))]

    def gather_second(piece, i, first):
        copies = []
        for n, to in enumerate((1, -1)):
            first[n].wait_recv()
            copies.append(send(piece(-to), piece(-to), ag_s.at[i, 2 + n], ag_r.at[i, 2 + n], at_y(to)))
        return copies

    def gather_third(piece, i, second):
        copies = []
        for n, to in enumerate((1, -1)):
            second[n].wait_recv()
            copies.append(send(piece(-2 * to), piece(-2 * to), ag_s.at[i, 4 + n], ag_r.at[i, 4 + n], at_y(to)))
        over = piece(-2 * side)
        return copies + [send(over, over, ag_s.at[i, 6], ag_r.at[i, 6], at_y(2 * side))]

    def share(half, i, far):
        settle(far)
        return send(half, half, fw_s.at[i], fw_r.at[i], mate)

    def spread_top(s):
        @pl.when(p == s)
        def _():
            tsrc[s] = jnp.concatenate([a[0, k].T for k in range(KB)], axis=0).reshape(ST, 2, NY, SL, W)
            for t in range(2 * NY):
                src, dst = tsrc.at[s, :, t % 2, t // 2], tt.at[s, :, t % 2, t // 2]
                if t == s:
                    tt[s, :, t % 2, t // 2] = tsrc[s, :, t % 2, t // 2]
                else:
                    pltpu.make_async_remote_copy(src_ref=src, dst_ref=dst, send_sem=ts_s.at[s, t], recv_sem=ts_r.at[s],
                                                 device_id=(t, q), device_id_type=MESH).start()

    def gather_top(s):
        here = tt.at[s, :, c, y]

        @pl.when(p != s)
        def _():
            pltpu.make_async_remote_copy(src_ref=here, dst_ref=here, send_sem=ts_s.at[s, 0], recv_sem=ts_r.at[s],
                                         device_id=mate, device_id_type=MESH).wait_recv()
        return gather_first(top_piece(s), 3 * s + 2)

    def swap(s, j, tops):
        mask = onehot(j, piv_ref[s:s + 1, :])
        taken = jnp.sum(jnp.where(mask, 1.0, 0.0), axis=1, keepdims=True) > 0.0
        hot = as_hot(mask)
        new = []
        for k in range(KB):
            hi, lo = split(tops[k * W:(k + 1) * W])
            new.append(jnp.where(taken, dot(hot, hi, 1, 1) + dot(hot, lo, 1, 1), a[j, k]))
        return new

    def below(s, j):
        return split(lg[s, W:, :] if j else jnp.where(p > s, lg[s, :W, :], 0.0))

    def update(j):
        new = swap(0, j, tt[0].reshape(KB * W, W))
        low = below(0, j)
        upper = ut[0].reshape(KB * W, W)
        for k in range(KB):
            a[j, k] = new[k] - dot3(low, split(upper[k * W:(k + 1) * W]))

    lined = jnp.logical_or(q == HOLDERS[0], q == HOLDERS[1])

    def rows_first():
        @pl.when(lined)
        def _():
            hot = [as_hot(onehot(j, piv_ref[1:2, :])) for j in range(2)]
            total = jnp.zeros((W, W), jnp.float32)
            for j in range(2):
                for part in split(loc[j * W:(j + 1) * W, :]):
                    total = total + dot(hot[j], part, 0, 0)
            et[...] = total.reshape(2, NY, PR, W)
            remote(et.at[1 - c], ep, e_s.at[0], e_r.at[0], mate).start()

            @pl.when(p == 1)
            def _():
                for t in range(2 * NY):
                    piece = pl.ds((t % 2) * NY * PR + (t // 2) * PR, PR)
                    if t == 1:
                        ms[1] = loc[piece, :]
                    else:
                        remote(loc.at[piece], ms.at[1], n_s.at[t], n_r, (t, q)).start()

    def rows_second():
        @pl.when(lined)
        def _():
            remote(et.at[1 - c], ep, e_s.at[0], e_r.at[0], mate).wait_recv()
            es[...] = et[c] + ep[...]
            for i in range(1, NY):
                remote(es.at[chip(i)], er.at[i - 1], e_s.at[i], e_r.at[i], at_y(i)).start()

    def rows_third():
        @pl.when(lined)
        def _():
            total = es[y]
            for i in range(1, NY):
                remote(es.at[chip(i)], er.at[i - 1], e_s.at[i], e_r.at[i], at_y(i)).wait_recv()
                total = total + er[i - 1]
            ms[0] = total

            @pl.when(p != 1)
            def _():
                remote(ms.at[1], ms.at[1], n_s.at[0], n_r, mate).wait_recv()
        for n in range(2):
            @pl.when(q == HOLDERS[n])
            def _():
                mr[n] = ms[...]
                for i in range(1, NX):
                    remote(mr.at[n], mr.at[n], m_s.at[i], m_r.at[n], at_x(i)).start()

    def rows_fourth():
        for n in range(2):
            @pl.when(z == HOLDERS[n] % NZ)
            def _():
                @pl.when(q != HOLDERS[n])
                def _():
                    remote(mr.at[n], mr.at[n], m_s.at[0], m_r.at[n], mate).wait_recv()
                for i in range(1, NZ):
                    remote(mr.at[n], mr.at[n], m_s.at[NX + i], m_r.at[n], at_z(i)).start()

    def rows_here():
        for n in range(2):
            @pl.when(z != HOLDERS[n] % NZ)
            def _():
                remote(mr.at[n], mr.at[n], m_s.at[0], m_r.at[n], mate).wait_recv()
        mn[:, c, y] = jnp.where(own_ref[0] == HOLDERS[0], mr[0], mr[1])

    def rows_piece(step):
        return mn.at[:, c, chip(step)]

    def rows_near(i):
        return [send(rows_piece(0), rows_piece(0), ag_s.at[i, n], ag_r.at[i, n], at_y(to))
                for n, to in enumerate((2, -2, 1, -1))]

    def rows_far(i, near):
        copies = near[2:]
        for n, to in enumerate((1, -1)):
            near[n].wait_recv()
            piece = rows_piece(-2 * to)
            copies.append(send(piece, piece, ag_s.at[i, 4 + n], ag_r.at[i, 4 + n], at_y(to)))
        over = rows_piece(-2 * side)
        return copies + [send(over, over, ag_s.at[i, 6], ag_r.at[i, 6], at_y(2 * side))]

    every = [(s, h) for s in range(2) for h in range(ST)]
    slot = {(s, h): 3 * s + h for s, h in every}

    pairs = {(0, h): pair_up(0, h) for h in range(ST)}
    rows_first()

    first = jnp.broadcast_to(piv_ref[0:1, :].astype(jnp.float32), (W, W)).T
    hit = jnp.where(first == piv_ref[1:2, :].astype(jnp.float32), 1.0, 0.0)
    place = jnp.sum(hit * lax.broadcasted_iota(jnp.int32, (W, W), 0).astype(jnp.float32), axis=0, keepdims=True)
    moved = jnp.sum(hit, axis=0, keepdims=True) > 0.0
    pt[1] = pick(jnp.where(moved, place.astype(jnp.int32), piv_ref[1:2, :]))
    pairs.update({(1, h): pair_up(1, h) for h in range(ST)})

    rows_second()
    work = {k: reduce_first(*k, pairs[k]) for k in every}
    for n in range(len(HOLDERS)):
        scatter(n)
    for s in range(2):
        spread_top(s)
    rows_third()
    work = {k: reduce_second(*k, work[k]) for k in every}
    rows_fourth()
    for n in range(len(HOLDERS)):
        arrived(n)
    z_copies = [gather_z(i) for i in range(2)]
    work = {k: reduce_third(*k, work[k]) for k in every}
    tops = [gather_top(s) for s in range(2)]
    upper = {}
    for k in every:
        solve(*k, work[k])
        upper[k] = gather_first(upper_piece(*k), slot[k])
    rows_here()
    rows = rows_near(6)
    tops = [gather_second(top_piece(s), 3 * s + 2, tops[s]) for s in range(2)]
    upper = {k: gather_second(upper_piece(*k), slot[k], upper[k]) for k in every}
    x_copies = []
    settle(z_copies[0])
    x_copies.append(gather_x(0))
    rows = rows_far(6, rows)
    tops = [gather_third(top_piece(s), 3 * s + 2, tops[s]) for s in range(2)]
    upper = {k: gather_third(upper_piece(*k), slot[k], upper[k]) for k in every}
    settle(z_copies[1])
    x_copies.append(gather_x(1))
    rows = share(mn.at[:, c], 6, rows)
    upper = {k: share(ut.at[k[0], k[1], c], slot[k], upper[k]) for k in every}
    tops = [share(tt.at[s, :, c], 3 * s + 2, tops[s]) for s in range(2)]

    for h in range(ST):
        upper[0, h].wait_recv()
    solved = [split(ut[0, h].reshape(WIDE, W)) for h in range(ST)]
    rows.wait_recv()
    mixed = split(lax.dot_general(inv_ref[1], mn[0].reshape(W, W), (((1,), (0,)), ((), ())),
                                  precision=lax.Precision.HIGHEST, preferred_element_type=jnp.float32))
    drop = [dot3(solved[h], mixed) for h in range(ST)]
    second = split(mn[1].reshape(W, W))
    drop_top = [dot3(solved[h], second) for h in range(ST)]
    settle(x_copies[0])
    tops[0].wait_recv()
    for j in range(2):
        update(j)

    @pl.when(p == 0)
    def _():
        whole = ut[0].reshape(KB * W, W)
        for k in range(KB):
            a[0, k] = whole[k * W:(k + 1) * W].T

    ids = lax.broadcasted_iota(jnp.int32, (W, W), 1) + W
    link = first == ids.astype(jnp.float32)
    linked = jnp.sum(jnp.where(link, 1.0, 0.0), axis=0, keepdims=True) > 0.0
    link = as_hot(link)
    tops[1].wait_recv()
    for h in range(ST):
        hi, lo = split(tt[0, h].reshape(WIDE, W))
        raw = jnp.where(linked, dot(hi, link, 1, 0) + dot(lo, link, 1, 0), tt[1, h].reshape(WIDE, W))
        t1[h * WIDE:(h + 1) * WIDE, :] = raw - drop_top[h]
    for j in range(2):
        for k, block in enumerate(swap(1, j, t1[...])):
            o_buf[j, k] = block
    settle(x_copies[1])
    low = [below(1, j) for j in range(2)]
    for h in range(ST):
        upper[1, h].wait_recv()
        solved1 = ut[1, h].reshape(WIDE, W) - drop[h]
        u1[h * WIDE:(h + 1) * WIDE, :] = solved1
        solved1 = split(solved1)
        for j in range(2):
            product = dot3(low[j], solved1)
            at = h * (W // 2)
            part = pl.ds(at, W // 2)
            o_buf[j, 2 * h] = o_buf[j, 2 * h] - product[:, at:at + W]
            rest = product[:, :W // 2] if h else product[:, W:]
            o_buf[j, 1, :, part] = o_buf[j, 1, :, part] - rest

    @pl.when(p == 1)
    def _():
        for k in range(KB):
            o_buf[0, k] = u1[k * W:(k + 1) * W, :].T

    store = pltpu.make_async_copy(o_buf, o_hbm, out_sem)
    store.start()
    for copy in sent:
        copy.wait_send()
    for s in range(2):
        @pl.when(p == s)
        def _():
            for t in range(2 * NY):
                if t != s:
                    piece = tsrc.at[s, :, t % 2, t // 2]
                    pltpu.make_async_remote_copy(src_ref=piece, dst_ref=piece, send_sem=ts_s.at[s, t],
                                                 recv_sem=ts_r.at[s], device_id=mate, device_id_type=MESH).wait_send()
    for n, h in enumerate(HOLDERS):
        @pl.when(q == h)
        def _():
            @pl.loop(1, NQ)
            def _(i):
                piece = loc.at[pl.ds(0, PR)]
                pltpu.make_async_remote_copy(src_ref=piece, dst_ref=piece, send_sem=sc_s.at[i], recv_sem=sc_r.at[n],
                                             device_id=mate, device_id_type=MESH).wait_send()

    @pl.when(lined)
    def _():
        remote(et.at[1 - c], ep, e_s.at[0], e_r.at[0], mate).wait_send()
        for i in range(1, NY):
            remote(es.at[chip(i)], er.at[i - 1], e_s.at[i], e_r.at[i], at_y(i)).wait_send()

        @pl.when(p == 1)
        def _():
            for t in range(2 * NY):
                if t != 1:
                    remote(loc.at[pl.ds(0, PR)], ms.at[1], n_s.at[t], n_r, mate).wait_send()

    for n in range(2):
        @pl.when(q == HOLDERS[n])
        def _():
            for i in range(1, NX):
                remote(mr.at[n], mr.at[n], m_s.at[i], m_r.at[n], mate).wait_send()

        @pl.when(z == HOLDERS[n] % NZ)
        def _():
            for i in range(1, NZ):
                remote(mr.at[n], mr.at[n], m_s.at[NX + i], m_r.at[n], mate).wait_send()
    store.wait()


def body(matrix, lower_panel, inverses, pivots, panel_owner):
    f32 = jnp.float32
    dma = pltpu.SemaphoreType.DMA
    blocks = matrix.transpose(0, 2, 1, 3)
    any_spec = pl.BlockSpec(memory_space=pl.ANY)
    line = (ST, 2, NY, SL, W)
    out = pl.pallas_call(
        kernel,
        out_shape=jax.ShapeDtypeStruct(blocks.shape, f32),
        in_specs=[any_spec] * 5,
        out_specs=any_spec,
        scratch_shapes=[
            pltpu.VMEM((2, KB, W, W), f32),
            pltpu.VMEM((2 * W, W), f32),
            pltpu.VMEM((2, W, W), f32),
            pltpu.VMEM((2, W), jnp.int32),
            pltpu.SMEM((2,), jnp.int32),
            pltpu.VMEM((2,) + line, f32),
            pltpu.VMEM((2, ST, NY, SL, W), f32),
            pltpu.VMEM((2, ST, NY, SL, W), f32),
            pltpu.VMEM((2, ST, 3, SL, W), f32),
            pltpu.VMEM((2, ST, 2, SL, W), f32),
            pltpu.VMEM((2, ST, 2, SL, W), f32),
            pltpu.VMEM((2, ST, 2, SL, W), f32),
            pltpu.VMEM((2, ST, 2, SL, W), f32),
            pltpu.VMEM((2,) + line, f32),
            pltpu.VMEM((2,) + line, f32),
            pltpu.VMEM((2,) + line, f32),
            pltpu.VMEM((3, PR, W), f32),
            pltpu.VMEM((2, 2 * W, W), f32),
            pltpu.VMEM((2, NY, PR, W), f32),
            pltpu.VMEM((NY, PR, W), f32),
            pltpu.VMEM((NY, PR, W), f32),
            pltpu.VMEM((NY - 1, PR, W), f32),
            pltpu.VMEM((2, PR, W), f32),
            pltpu.VMEM((2, 2, PR, W), f32),
            pltpu.VMEM((2, 2, NY, PR, W), f32),
            pltpu.VMEM((KB * W, W), f32),
            pltpu.VMEM((KB * W, W), f32),
            pltpu.VMEM((2, KB, W, W), f32),
            dma((5,)), dma(()),
            dma((2, ST)), dma((2, ST)),
            dma((2, ST, 7)), dma((2, ST, 7)),
            dma((2, 2 * NY)), dma((2,)),
            dma((7, 7)), dma((7, 7)),
            dma((7,)), dma((7,)),
            dma((NQ,)), dma((3,)),
            dma((2, NZ)), dma((2, NZ)),
            dma((2, NX)), dma((2, NX)),
            dma((NY,)), dma((NY,)),
            dma((2 * NY,)), dma(()),
            dma((NX + NZ,)), dma((2,)),
        ],
        compiler_params=pltpu.CompilerParams(collective_id=0, has_side_effects=True, vmem_limit_bytes=60 * 2**20),
    )(blocks, lower_panel.reshape(2 * W, W), inverses, pivots, panel_owner)
    return out.transpose(0, 2, 1, 3)


def solution(mesh):
    in_specs = (P(None, "prow", None, "pcol"), P(None, "prow", "pcol"), P(), P(), P())
    return jax.shard_map(body, mesh=mesh, in_specs=in_specs, out_specs=P(None, "prow", None, "pcol"), check_vma=False)
```

```python
import jax
import jax.numpy as jnp
from jax import lax
from jax.experimental import pallas as pl
from jax.experimental.pallas import tpu as pltpu
from jax.sharding import PartitionSpec as P

MESH = pl.DeviceIdType.MESH
W = 256
KB = 3
NY = 8
ST = 2
SL = 24
WIDE = 2 * NY * SL
NX, NZ = 4, 8
NQ = NX * NZ
PR = 16
HOLDERS = (30, 31, 0)


def split(x):
    hi = x.astype(jnp.bfloat16)
    return hi, (x - hi.astype(jnp.float32)).astype(jnp.bfloat16)


def dot(a, b, ca, cb):
    return lax.dot_general(a, b, (((ca,), (cb,)), ((), ())), preferred_element_type=jnp.float32)


def dot3(a, b):
    return dot(a[0], b[0], 1, 1) + dot(a[0], b[1], 1, 1) + dot(a[1], b[0], 1, 1)


def as_hot(mask):
    return jnp.where(mask, 1.0, 0.0).astype(jnp.bfloat16)


def kernel(a_hbm, l_hbm, inv_hbm, piv_hbm, own_hbm, o_hbm, a, loc, inv_ref, piv_ref, own_ref, pt, pair, s_buf, f_buf,
           b_buf, g_buf, d_buf, r_buf, ut, tt, tsrc, lp, lg, et, ep, es, er, ms, mr, mn, t1, u1, o_buf, load_sem, out_sem, pair_s,
           pair_r, rs_s, rs_r, ts_s, ts_r, ag_s, ag_r, fw_s, fw_r, sc_s, sc_r, z_s, z_r, x_s, x_r, e_s, e_r, n_s, n_r,
           m_s, m_r):
    p, q = lax.axis_index("prow"), lax.axis_index("pcol")
    y, c = p // 2, p % 2
    x, z = q // NZ, q % NZ
    side = 1 - 2 * c

    def chip(step):
        return lax.rem(y + step + 2 * NY, NY)

    def at_y(step):
        return (chip(step) * 2 + c, q)

    mate = (y * 2 + 1 - c, q)

    def at_x(step):
        return (p, lax.rem(x + step, NX) * NZ + z)

    def at_z(step):
        return (p, x * NZ + lax.rem(z + step, NZ))

    sent = []

    def remote(src, dst, s, r, to):
        return pltpu.make_async_remote_copy(src_ref=src, dst_ref=dst, send_sem=s, recv_sem=r, device_id=to,
                                            device_id_type=MESH)

    def send(src, dst, s, r, to):
        copy = remote(src, dst, s, r, to)
        copy.start()
        sent.append(copy)
        return copy

    def settle(copies):
        for copy in copies:
            copy.wait_recv()

    load_a = pltpu.make_async_copy(a_hbm, a, load_sem.at[0])
    load_p = pltpu.make_async_copy(piv_hbm, piv_ref, load_sem.at[1])
    load_rest = [pltpu.make_async_copy(src, dst, load_sem.at[2 + i]) for i, (src, dst) in enumerate(
        ((l_hbm, loc), (inv_hbm, inv_ref), (own_hbm, own_ref)))]
    for copy in [load_p, load_a] + load_rest:
        copy.start()

    barrier = pltpu.get_barrier_semaphore()
    for h in HOLDERS:
        @pl.when(q != h)
        def _():
            pl.semaphore_signal(barrier, inc=1, device_id=(p, h), device_id_type=MESH)
    greet = [at_y(i) for i in range(1, NY)] + [mate] + [at_z(i) for i in range(1, NZ)] + [at_x(i) for i in range(1, NX)]
    for to in greet:
        pl.semaphore_signal(barrier, inc=1, device_id=to, device_id_type=MESH)

    @pl.when(y != 0)
    def _():
        pl.semaphore_signal(barrier, inc=1, device_id=(1 - c, q), device_id_type=MESH)

    def onehot(j, wanted):
        rows = lax.broadcasted_iota(jnp.int32, (W, W), 0) + (j * 2 * NY + p) * W
        return rows == wanted

    def pick(wanted):
        hot = [as_hot(onehot(j, wanted)) for j in range(2)]
        blocks = []
        for k in range(KB):
            total = jnp.zeros((W, W), jnp.float32)
            for j in range(2):
                for part in split(a[j, k]):
                    total = total + dot(part, hot[j], 0, 0)
            blocks.append(total)
        return jnp.concatenate(blocks, axis=0).reshape(ST, 2, NY, SL, W)

    load_p.wait()
    load_a.wait()
    pt[0] = pick(piv_ref[0:1, :])

    holds = jnp.logical_or(q == HOLDERS[0], jnp.logical_or(q == HOLDERS[1], q == HOLDERS[2]))
    heard = len(greet) + jnp.where(holds, NQ - 1, 0) + jnp.where(y == 0, NY - 1, 0)
    pl.semaphore_wait(barrier, heard)

    for copy in load_rest:
        copy.wait()

    def scatter(n):
        h = HOLDERS[n]

        @pl.when(q == h)
        def _():
            lp[n] = loc[h * PR:(h + 1) * PR, :]

            @pl.loop(1, NQ)
            def _(i):
                to = lax.rem(h + i, NQ)
                piece = pl.ds(pl.multiple_of(to * PR, 8), PR)
                pltpu.make_async_remote_copy(src_ref=loc.at[piece], dst_ref=lp.at[n], send_sem=sc_s.at[i],
                                             recv_sem=sc_r.at[n], device_id=(p, to), device_id_type=MESH).start()

    def arrived(n):
        @pl.when(q != HOLDERS[n])
        def _():
            pltpu.make_async_remote_copy(src_ref=lp.at[n], dst_ref=lp.at[n], send_sem=sc_s.at[0],
                                         recv_sem=sc_r.at[n], device_id=mate, device_id_type=MESH).wait_recv()

    l_rows = pl.ds(pl.multiple_of(q * PR, 8), PR)
    l_wide = pl.ds(pl.multiple_of(x * (NZ * PR), 8), NZ * PR)

    def gather_z(i):
        lg[i, l_rows, :] = jnp.where(own_ref[i] == HOLDERS[1], lp[1], lp[2 * i])
        piece = lg.at[i, l_rows]
        return [send(piece, piece, z_s.at[i, n], z_r.at[i, n], at_z(n)) for n in range(1, NZ)]

    def gather_x(i):
        piece = lg.at[i, l_wide]
        return [send(piece, piece, x_s.at[i, n], x_r.at[i, n], at_x(n)) for n in range(1, NX)]

    def pair_up(s, h):
        return send(pt.at[s, h, 1 - c], pair.at[s, h], pair_s.at[s, h], pair_r.at[s, h], mate)

    def reduce_first(s, h, pair_copy):
        pair_copy.wait_recv()
        s_buf[s, h] = pt[s, h, c] + pair[s, h]
        plan = ((-3, -1), (4, -2 * side), (3, 1))
        return [send(s_buf.at[s, h, chip(end)], f_buf.at[s, h, n], rs_s.at[s, h, n], rs_r.at[s, h, n], at_y(to))
                for n, (end, to) in enumerate(plan)]

    def reduce_second(s, h, first):
        settle(first)
        cross = f_buf[s, h, 1]
        b_buf[s, h, 0] = s_buf[s, h, chip(-2)] + f_buf[s, h, 0] + jnp.where(c == 0, cross, 0.0)
        b_buf[s, h, 1] = s_buf[s, h, chip(2)] + f_buf[s, h, 2] + jnp.where(c == 0, 0.0, cross)
        return [send(b_buf.at[s, h, n], g_buf.at[s, h, n], rs_s.at[s, h, 3 + n], rs_r.at[s, h, 3 + n], at_y(to))
                for n, to in enumerate((-1, 1))]

    def reduce_third(s, h, second):
        settle(second)
        d_buf[s, h, 0] = s_buf[s, h, chip(-1)] + g_buf[s, h, 0]
        d_buf[s, h, 1] = s_buf[s, h, chip(1)] + g_buf[s, h, 1]
        return [send(d_buf.at[s, h, n], r_buf.at[s, h, n], rs_s.at[s, h, 5 + n], rs_r.at[s, h, 5 + n], at_y(to))
                for n, to in enumerate((-1, 1))]

    def solve(s, h, last):
        settle(last)
        total = s_buf[s, h, y] + r_buf[s, h, 0] + r_buf[s, h, 1]
        ut[s, h, c, y] = lax.dot_general(total, inv_ref[s], (((1,), (1,)), ((), ())),
                                         precision=lax.Precision.HIGHEST, preferred_element_type=jnp.float32)

    def upper_piece(s, h):
        return lambda step: ut.at[s, h, c, chip(step)]

    def top_piece(s):
        return lambda step: tt.at[s, :, c, chip(step)]

    def gather_first(piece, i):
        return [send(piece(0), piece(0), ag_s.at[i, n], ag_r.at[i, n], at_y(to)) for n, to in enumerate((1, -1))]

    def gather_second(piece, i, first):
        copies = []
        for n, to in enumerate((1, -1)):
            first[n].wait_recv()
            copies.append(send(piece(-to), piece(-to), ag_s.at[i, 2 + n], ag_r.at[i, 2 + n], at_y(to)))
        return copies

    def gather_third(piece, i, second):
        copies = []
        for n, to in enumerate((1, -1)):
            second[n].wait_recv()
            copies.append(send(piece(-2 * to), piece(-2 * to), ag_s.at[i, 4 + n], ag_r.at[i, 4 + n], at_y(to)))
        over = piece(-2 * side)
        return copies + [send(over, over, ag_s.at[i, 6], ag_r.at[i, 6], at_y(2 * side))]

    def ring_third(piece, i, second):
        copies = []
        for n, to in enumerate((1, -1)):
            second[n].wait_recv()
            copies.append(send(piece(-2 * to), piece(-2 * to), ag_s.at[i, 4 + n], ag_r.at[i, 4 + n], at_y(to)))
        return copies

    def ring_fourth(piece, i, third):
        settle(third)
        last = piece(-3 * side)
        return [send(last, last, ag_s.at[i, 6], ag_r.at[i, 6], at_y(side))]

    def share(half, i, far):
        settle(far)
        return send(half, half, fw_s.at[i], fw_r.at[i], mate)

    def spread_top(s):
        @pl.when(p == s)
        def _():
            tsrc[s] = jnp.concatenate([a[0, k].T for k in range(KB)], axis=0).reshape(ST, 2, NY, SL, W)
            for t in range(2 * NY):
                src, dst = tsrc.at[s, :, t % 2, t // 2], tt.at[s, :, t % 2, t // 2]
                if t == s:
                    tt[s, :, t % 2, t // 2] = tsrc[s, :, t % 2, t // 2]
                else:
                    pltpu.make_async_remote_copy(src_ref=src, dst_ref=dst, send_sem=ts_s.at[s, t], recv_sem=ts_r.at[s],
                                                 device_id=(t, q), device_id_type=MESH).start()

    def gather_top(s):
        here = tt.at[s, :, c, y]

        @pl.when(p != s)
        def _():
            pltpu.make_async_remote_copy(src_ref=here, dst_ref=here, send_sem=ts_s.at[s, 0], recv_sem=ts_r.at[s],
                                         device_id=mate, device_id_type=MESH).wait_recv()
        return gather_first(top_piece(s), 3 * s + 2)

    def swap(s, j, tops):
        mask = onehot(j, piv_ref[s:s + 1, :])
        taken = jnp.sum(jnp.where(mask, 1.0, 0.0), axis=1, keepdims=True) > 0.0
        hot = as_hot(mask)
        new = []
        for k in range(KB):
            hi, lo = split(tops[k * W:(k + 1) * W])
            new.append(jnp.where(taken, dot(hot, hi, 1, 1) + dot(hot, lo, 1, 1), a[j, k]))
        return new

    def below(s, j):
        return split(lg[s, W:, :] if j else jnp.where(p > s, lg[s, :W, :], 0.0))

    def update(j):
        new = swap(0, j, tt[0].reshape(KB * W, W))
        low = below(0, j)
        upper = ut[0].reshape(KB * W, W)
        for k in range(KB):
            a[j, k] = new[k] - dot3(low, split(upper[k * W:(k + 1) * W]))

    lined = jnp.logical_or(q == HOLDERS[0], q == HOLDERS[1])

    def rows_first():
        @pl.when(lined)
        def _():
            hot = [as_hot(onehot(j, piv_ref[1:2, :])) for j in range(2)]
            total = jnp.zeros((W, W), jnp.float32)
            for j in range(2):
                for part in split(loc[j * W:(j + 1) * W, :]):
                    total = total + dot(hot[j], part, 0, 0)
            et[...] = total.reshape(2, NY, PR, W)
            remote(et.at[1 - c], ep, e_s.at[0], e_r.at[0], mate).start()

            @pl.when(p == 1)
            def _():
                for t in range(2 * NY):
                    piece = pl.ds((t % 2) * NY * PR + (t // 2) * PR, PR)
                    if t == 1:
                        ms[1] = loc[piece, :]
                    else:
                        remote(loc.at[piece], ms.at[1], n_s.at[t], n_r, (t, q)).start()

    def rows_second():
        @pl.when(lined)
        def _():
            remote(et.at[1 - c], ep, e_s.at[0], e_r.at[0], mate).wait_recv()
            es[...] = et[c] + ep[...]
            for i in range(1, NY):
                remote(es.at[chip(i)], er.at[i - 1], e_s.at[i], e_r.at[i], at_y(i)).start()

    def rows_third():
        @pl.when(lined)
        def _():
            total = es[y]
            for i in range(1, NY):
                remote(es.at[chip(i)], er.at[i - 1], e_s.at[i], e_r.at[i], at_y(i)).wait_recv()
                total = total + er[i - 1]
            ms[0] = total

            @pl.when(p != 1)
            def _():
                remote(ms.at[1], ms.at[1], n_s.at[0], n_r, mate).wait_recv()
        for n in range(2):
            @pl.when(q == HOLDERS[n])
            def _():
                mr[n] = ms[...]
                for i in range(1, NX):
                    remote(mr.at[n], mr.at[n], m_s.at[i], m_r.at[n], at_x(i)).start()

    def rows_fourth():
        for n in range(2):
            @pl.when(z == HOLDERS[n] % NZ)
            def _():
                @pl.when(q != HOLDERS[n])
                def _():
                    remote(mr.at[n], mr.at[n], m_s.at[0], m_r.at[n], mate).wait_recv()
                for i in range(1, NZ):
                    remote(mr.at[n], mr.at[n], m_s.at[NX + i], m_r.at[n], at_z(i)).start()

    def rows_here():
        for n in range(2):
            @pl.when(z != HOLDERS[n] % NZ)
            def _():
                remote(mr.at[n], mr.at[n], m_s.at[0], m_r.at[n], mate).wait_recv()
        mn[:, c, y] = jnp.where(own_ref[0] == HOLDERS[0], mr[0], mr[1])

    def rows_piece(step):
        return mn.at[:, c, chip(step)]

    def rows_near(i):
        return [send(rows_piece(0), rows_piece(0), ag_s.at[i, n], ag_r.at[i, n], at_y(to))
                for n, to in enumerate((2, -2, 1, -1))]

    def rows_far(i, near):
        copies = near[2:]
        for n, to in enumerate((1, -1)):
            near[n].wait_recv()
            piece = rows_piece(-2 * to)
            copies.append(send(piece, piece, ag_s.at[i, 4 + n], ag_r.at[i, 4 + n], at_y(to)))
        over = rows_piece(-2 * side)
        return copies + [send(over, over, ag_s.at[i, 6], ag_r.at[i, 6], at_y(2 * side))]

    every = [(s, h) for s in range(2) for h in range(ST)]
    slot = {(s, h): 3 * s + h for s, h in every}

    pairs = {(0, h): pair_up(0, h) for h in range(ST)}
    rows_first()

    first = jnp.broadcast_to(piv_ref[0:1, :].astype(jnp.float32), (W, W)).T
    hit = jnp.where(first == piv_ref[1:2, :].astype(jnp.float32), 1.0, 0.0)
    place = jnp.sum(hit * lax.broadcasted_iota(jnp.int32, (W, W), 0).astype(jnp.float32), axis=0, keepdims=True)
    moved = jnp.sum(hit, axis=0, keepdims=True) > 0.0
    pt[1] = pick(jnp.where(moved, place.astype(jnp.int32), piv_ref[1:2, :]))
    pairs.update({(1, h): pair_up(1, h) for h in range(ST)})

    rows_second()
    work = {k: reduce_first(*k, pairs[k]) for k in every}
    for n in range(len(HOLDERS)):
        scatter(n)
    for s in range(2):
        spread_top(s)
    rows_third()
    work = {k: reduce_second(*k, work[k]) for k in every}
    rows_fourth()
    for n in range(len(HOLDERS)):
        arrived(n)
    z_copies = [gather_z(i) for i in range(2)]
    work = {k: reduce_third(*k, work[k]) for k in every}
    tops = [gather_top(s) for s in range(2)]
    upper = {}
    for k in every:
        solve(*k, work[k])
        upper[k] = gather_first(upper_piece(*k), slot[k])
    rows_here()
    rows = rows_near(6)
    tops = [gather_second(top_piece(s), 3 * s + 2, tops[s]) for s in range(2)]
    upper = {k: gather_second(upper_piece(*k), slot[k], upper[k]) for k in every}
    x_copies = []
    settle(z_copies[0])
    x_copies.append(gather_x(0))
    rows = rows_far(6, rows)
    tops = [ring_third(top_piece(s), 3 * s + 2, tops[s]) for s in range(2)]
    upper = {k: gather_third(upper_piece(*k), slot[k], upper[k]) for k in every}
    tops = [ring_fourth(top_piece(s), 3 * s + 2, tops[s]) for s in range(2)]
    settle(z_copies[1])
    x_copies.append(gather_x(1))
    rows = share(mn.at[:, c], 6, rows)
    upper = {k: share(ut.at[k[0], k[1], c], slot[k], upper[k]) for k in every}
    tops = [share(tt.at[s, :, c], 3 * s + 2, tops[s]) for s in range(2)]

    for h in range(ST):
        upper[0, h].wait_recv()
    solved = [split(ut[0, h].reshape(WIDE, W)) for h in range(ST)]
    rows.wait_recv()
    mixed = split(lax.dot_general(inv_ref[1], mn[0].reshape(W, W), (((1,), (0,)), ((), ())),
                                  precision=lax.Precision.HIGHEST, preferred_element_type=jnp.float32))
    drop = [dot3(solved[h], mixed) for h in range(ST)]
    second = split(mn[1].reshape(W, W))
    drop_top = [dot3(solved[h], second) for h in range(ST)]
    settle(x_copies[0])
    tops[0].wait_recv()
    for j in range(2):
        update(j)

    @pl.when(p == 0)
    def _():
        whole = ut[0].reshape(KB * W, W)
        for k in range(KB):
            a[0, k] = whole[k * W:(k + 1) * W].T

    ids = lax.broadcasted_iota(jnp.int32, (W, W), 1) + W
    link = first == ids.astype(jnp.float32)
    linked = jnp.sum(jnp.where(link, 1.0, 0.0), axis=0, keepdims=True) > 0.0
    link = as_hot(link)
    tops[1].wait_recv()
    for h in range(ST):
        hi, lo = split(tt[0, h].reshape(WIDE, W))
        raw = jnp.where(linked, dot(hi, link, 1, 0) + dot(lo, link, 1, 0), tt[1, h].reshape(WIDE, W))
        t1[h * WIDE:(h + 1) * WIDE, :] = raw - drop_top[h]
    for j in range(2):
        for k, block in enumerate(swap(1, j, t1[...])):
            o_buf[j, k] = block
    settle(x_copies[1])
    low = [below(1, j) for j in range(2)]
    for h in range(ST):
        upper[1, h].wait_recv()
        solved1 = ut[1, h].reshape(WIDE, W) - drop[h]
        u1[h * WIDE:(h + 1) * WIDE, :] = solved1
        solved1 = split(solved1)
        for j in range(2):
            product = dot3(low[j], solved1)
            at = h * (W // 2)
            part = pl.ds(at, W // 2)
            o_buf[j, 2 * h] = o_buf[j, 2 * h] - product[:, at:at + W]
            rest = product[:, :W // 2] if h else product[:, W:]
            o_buf[j, 1, :, part] = o_buf[j, 1, :, part] - rest

    @pl.when(p == 1)
    def _():
        for k in range(KB):
            o_buf[0, k] = u1[k * W:(k + 1) * W, :].T

    store = pltpu.make_async_copy(o_buf, o_hbm, out_sem)
    store.start()
    for copy in sent:
        copy.wait_send()
    for s in range(2):
        @pl.when(p == s)
        def _():
            for t in range(2 * NY):
                if t != s:
                    piece = tsrc.at[s, :, t % 2, t // 2]
                    pltpu.make_async_remote_copy(src_ref=piece, dst_ref=piece, send_sem=ts_s.at[s, t],
                                                 recv_sem=ts_r.at[s], device_id=mate, device_id_type=MESH).wait_send()
    for n, h in enumerate(HOLDERS):
        @pl.when(q == h)
        def _():
            @pl.loop(1, NQ)
            def _(i):
                piece = loc.at[pl.ds(0, PR)]
                pltpu.make_async_remote_copy(src_ref=piece, dst_ref=piece, send_sem=sc_s.at[i], recv_sem=sc_r.at[n],
                                             device_id=mate, device_id_type=MESH).wait_send()

    @pl.when(lined)
    def _():
        remote(et.at[1 - c], ep, e_s.at[0], e_r.at[0], mate).wait_send()
        for i in range(1, NY):
            remote(es.at[chip(i)], er.at[i - 1], e_s.at[i], e_r.at[i], at_y(i)).wait_send()

        @pl.when(p == 1)
        def _():
            for t in range(2 * NY):
                if t != 1:
                    remote(loc.at[pl.ds(0, PR)], ms.at[1], n_s.at[t], n_r, mate).wait_send()

    for n in range(2):
        @pl.when(q == HOLDERS[n])
        def _():
            for i in range(1, NX):
                remote(mr.at[n], mr.at[n], m_s.at[i], m_r.at[n], mate).wait_send()

        @pl.when(z == HOLDERS[n] % NZ)
        def _():
            for i in range(1, NZ):
                remote(mr.at[n], mr.at[n], m_s.at[NX + i], m_r.at[n], mate).wait_send()
    store.wait()


def body(matrix, lower_panel, inverses, pivots, panel_owner):
    f32 = jnp.float32
    dma = pltpu.SemaphoreType.DMA
    blocks = matrix.transpose(0, 2, 1, 3)
    any_spec = pl.BlockSpec(memory_space=pl.ANY)
    line = (ST, 2, NY, SL, W)
    out = pl.pallas_call(
        kernel,
        out_shape=jax.ShapeDtypeStruct(blocks.shape, f32),
        in_specs=[any_spec] * 5,
        out_specs=any_spec,
        scratch_shapes=[
            pltpu.VMEM((2, KB, W, W), f32),
            pltpu.VMEM((2 * W, W), f32),
            pltpu.VMEM((2, W, W), f32),
            pltpu.VMEM((2, W), jnp.int32),
            pltpu.SMEM((2,), jnp.int32),
            pltpu.VMEM((2,) + line, f32),
            pltpu.VMEM((2, ST, NY, SL, W), f32),
            pltpu.VMEM((2, ST, NY, SL, W), f32),
            pltpu.VMEM((2, ST, 3, SL, W), f32),
            pltpu.VMEM((2, ST, 2, SL, W), f32),
            pltpu.VMEM((2, ST, 2, SL, W), f32),
            pltpu.VMEM((2, ST, 2, SL, W), f32),
            pltpu.VMEM((2, ST, 2, SL, W), f32),
            pltpu.VMEM((2,) + line, f32),
            pltpu.VMEM((2,) + line, f32),
            pltpu.VMEM((2,) + line, f32),
            pltpu.VMEM((3, PR, W), f32),
            pltpu.VMEM((2, 2 * W, W), f32),
            pltpu.VMEM((2, NY, PR, W), f32),
            pltpu.VMEM((NY, PR, W), f32),
            pltpu.VMEM((NY, PR, W), f32),
            pltpu.VMEM((NY - 1, PR, W), f32),
            pltpu.VMEM((2, PR, W), f32),
            pltpu.VMEM((2, 2, PR, W), f32),
            pltpu.VMEM((2, 2, NY, PR, W), f32),
            pltpu.VMEM((KB * W, W), f32),
            pltpu.VMEM((KB * W, W), f32),
            pltpu.VMEM((2, KB, W, W), f32),
            dma((5,)), dma(()),
            dma((2, ST)), dma((2, ST)),
            dma((2, ST, 7)), dma((2, ST, 7)),
            dma((2, 2 * NY)), dma((2,)),
            dma((7, 7)), dma((7, 7)),
            dma((7,)), dma((7,)),
            dma((NQ,)), dma((3,)),
            dma((2, NZ)), dma((2, NZ)),
            dma((2, NX)), dma((2, NX)),
            dma((NY,)), dma((NY,)),
            dma((2 * NY,)), dma(()),
            dma((NX + NZ,)), dma((2,)),
        ],
        compiler_params=pltpu.CompilerParams(collective_id=0, has_side_effects=True, vmem_limit_bytes=60 * 2**20),
    )(blocks, lower_panel.reshape(2 * W, W), inverses, pivots, panel_owner)
    return out.transpose(0, 2, 1, 3)


def solution(mesh):
    in_specs = (P(None, "prow", None, "pcol"), P(None, "prow", "pcol"), P(), P(), P())
    return jax.shard_map(body, mesh=mesh, in_specs=in_specs, out_specs=P(None, "prow", None, "pcol"), check_vma=False)
```

```python
import jax
import jax.numpy as jnp
from jax import lax
from jax.experimental import pallas as pl
from jax.experimental.pallas import tpu as pltpu
from jax.sharding import PartitionSpec as P

MESH = pl.DeviceIdType.MESH
W = 256
KB = 3
NY = 8
ST = 2
SL = 24
WIDE = 2 * NY * SL
NX, NZ = 4, 8
NQ = NX * NZ
PR = 16
HOLDERS = (30, 31, 0)


def split(x):
    hi = x.astype(jnp.bfloat16)
    return hi, (x - hi.astype(jnp.float32)).astype(jnp.bfloat16)


def dot(a, b, ca, cb):
    return lax.dot_general(a, b, (((ca,), (cb,)), ((), ())), preferred_element_type=jnp.float32)


def dot3(a, b):
    return dot(a[0], b[0], 1, 1) + dot(a[0], b[1], 1, 1) + dot(a[1], b[0], 1, 1)


def as_hot(mask):
    return jnp.where(mask, 1.0, 0.0).astype(jnp.bfloat16)


def kernel(a_hbm, l_hbm, inv_hbm, piv_hbm, own_hbm, o_hbm, a, loc, inv_ref, piv_ref, own_ref, pt, pair, s_buf, f_buf,
           b_buf, g_buf, d_buf, r_buf, ut, tt, tsrc, lp, lg, et, ep, es, er, ms, mr, mn, t1, u1, o_buf, load_sem, out_sem, pair_s,
           pair_r, rs_s, rs_r, ts_s, ts_r, ag_s, ag_r, fw_s, fw_r, sc_s, sc_r, z_s, z_r, x_s, x_r, e_s, e_r, n_s, n_r,
           m_s, m_r):
    p, q = lax.axis_index("prow"), lax.axis_index("pcol")
    y, c = p // 2, p % 2
    x, z = q // NZ, q % NZ
    side = 1 - 2 * c

    def chip(step):
        return lax.rem(y + step + 2 * NY, NY)

    def at_y(step):
        return (chip(step) * 2 + c, q)

    mate = (y * 2 + 1 - c, q)

    def at_x(step):
        return (p, lax.rem(x + step, NX) * NZ + z)

    def at_z(step):
        return (p, x * NZ + lax.rem(z + step, NZ))

    sent = []

    def remote(src, dst, s, r, to):
        return pltpu.make_async_remote_copy(src_ref=src, dst_ref=dst, send_sem=s, recv_sem=r, device_id=to,
                                            device_id_type=MESH)

    def send(src, dst, s, r, to):
        copy = remote(src, dst, s, r, to)
        copy.start()
        sent.append(copy)
        return copy

    def settle(copies):
        for copy in copies:
            copy.wait_recv()

    load_a = [pltpu.make_async_copy(a_hbm.at[:, k], a.at[:, k], load_sem.at[4 + k]) for k in range(KB)]
    load_p = pltpu.make_async_copy(piv_hbm, piv_ref, load_sem.at[0])
    load_rest = [pltpu.make_async_copy(src, dst, load_sem.at[1 + i]) for i, (src, dst) in enumerate(
        ((l_hbm, loc), (inv_hbm, inv_ref), (own_hbm, own_ref)))]
    for copy in [load_p] + load_a + load_rest:
        copy.start()

    barrier = pltpu.get_barrier_semaphore()
    for h in HOLDERS:
        @pl.when(q != h)
        def _():
            pl.semaphore_signal(barrier, inc=1, device_id=(p, h), device_id_type=MESH)
    greet = [at_y(i) for i in range(1, NY)] + [mate] + [at_z(i) for i in range(1, NZ)] + [at_x(i) for i in range(1, NX)]
    for to in greet:
        pl.semaphore_signal(barrier, inc=1, device_id=to, device_id_type=MESH)

    @pl.when(y != 0)
    def _():
        pl.semaphore_signal(barrier, inc=1, device_id=(1 - c, q), device_id_type=MESH)

    def onehot(j, wanted):
        rows = lax.broadcasted_iota(jnp.int32, (W, W), 0) + (j * 2 * NY + p) * W
        return rows == wanted

    def pick(wanted, loads=()):
        hot = [as_hot(onehot(j, wanted)) for j in range(2)]
        blocks = []
        for k in range(KB):
            for copy in loads[k:k + 1]:
                copy.wait()
            total = jnp.zeros((W, W), jnp.float32)
            for j in range(2):
                for part in split(a[j, k]):
                    total = total + dot(part, hot[j], 0, 0)
            blocks.append(total)
        return jnp.concatenate(blocks, axis=0).reshape(ST, 2, NY, SL, W)

    load_p.wait()
    pt[0] = pick(piv_ref[0:1, :], load_a)

    holds = jnp.logical_or(q == HOLDERS[0], jnp.logical_or(q == HOLDERS[1], q == HOLDERS[2]))
    heard = len(greet) + jnp.where(holds, NQ - 1, 0) + jnp.where(y == 0, NY - 1, 0)
    pl.semaphore_wait(barrier, heard)

    for copy in load_rest:
        copy.wait()

    def scatter(n):
        h = HOLDERS[n]

        @pl.when(q == h)
        def _():
            lp[n] = loc[h * PR:(h + 1) * PR, :]

            @pl.loop(1, NQ)
            def _(i):
                to = lax.rem(h + i, NQ)
                piece = pl.ds(pl.multiple_of(to * PR, 8), PR)
                pltpu.make_async_remote_copy(src_ref=loc.at[piece], dst_ref=lp.at[n], send_sem=sc_s.at[i],
                                             recv_sem=sc_r.at[n], device_id=(p, to), device_id_type=MESH).start()

    def arrived(n):
        @pl.when(q != HOLDERS[n])
        def _():
            pltpu.make_async_remote_copy(src_ref=lp.at[n], dst_ref=lp.at[n], send_sem=sc_s.at[0],
                                         recv_sem=sc_r.at[n], device_id=mate, device_id_type=MESH).wait_recv()

    l_rows = pl.ds(pl.multiple_of(q * PR, 8), PR)
    l_wide = pl.ds(pl.multiple_of(x * (NZ * PR), 8), NZ * PR)

    def gather_z(i):
        lg[i, l_rows, :] = jnp.where(own_ref[i] == HOLDERS[1], lp[1], lp[2 * i])
        piece = lg.at[i, l_rows]
        return [send(piece, piece, z_s.at[i, n], z_r.at[i, n], at_z(n)) for n in range(1, NZ)]

    def gather_x(i):
        piece = lg.at[i, l_wide]
        return [send(piece, piece, x_s.at[i, n], x_r.at[i, n], at_x(n)) for n in range(1, NX)]

    def pair_up(s, h):
        return send(pt.at[s, h, 1 - c], pair.at[s, h], pair_s.at[s, h], pair_r.at[s, h], mate)

    def reduce_first(s, h, pair_copy):
        pair_copy.wait_recv()
        s_buf[s, h] = pt[s, h, c] + pair[s, h]
        plan = ((-3, -1), (4, -2 * side), (3, 1))
        return [send(s_buf.at[s, h, chip(end)], f_buf.at[s, h, n], rs_s.at[s, h, n], rs_r.at[s, h, n], at_y(to))
                for n, (end, to) in enumerate(plan)]

    def reduce_second(s, h, first):
        settle(first)
        cross = f_buf[s, h, 1]
        b_buf[s, h, 0] = s_buf[s, h, chip(-2)] + f_buf[s, h, 0] + jnp.where(c == 0, cross, 0.0)
        b_buf[s, h, 1] = s_buf[s, h, chip(2)] + f_buf[s, h, 2] + jnp.where(c == 0, 0.0, cross)
        return [send(b_buf.at[s, h, n], g_buf.at[s, h, n], rs_s.at[s, h, 3 + n], rs_r.at[s, h, 3 + n], at_y(to))
                for n, to in enumerate((-1, 1))]

    def reduce_third(s, h, second):
        settle(second)
        d_buf[s, h, 0] = s_buf[s, h, chip(-1)] + g_buf[s, h, 0]
        d_buf[s, h, 1] = s_buf[s, h, chip(1)] + g_buf[s, h, 1]
        return [send(d_buf.at[s, h, n], r_buf.at[s, h, n], rs_s.at[s, h, 5 + n], rs_r.at[s, h, 5 + n], at_y(to))
                for n, to in enumerate((-1, 1))]

    def solve(s, h, last):
        settle(last)
        total = s_buf[s, h, y] + r_buf[s, h, 0] + r_buf[s, h, 1]
        ut[s, h, c, y] = lax.dot_general(total, inv_ref[s], (((1,), (1,)), ((), ())),
                                         precision=lax.Precision.HIGHEST, preferred_element_type=jnp.float32)

    def upper_piece(s, h):
        return lambda step: ut.at[s, h, c, chip(step)]

    def top_piece(s):
        return lambda step: tt.at[s, :, c, chip(step)]

    def gather_first(piece, i):
        return [send(piece(0), piece(0), ag_s.at[i, n], ag_r.at[i, n], at_y(to)) for n, to in enumerate((1, -1))]

    def gather_second(piece, i, first):
        copies = []
        for n, to in enumerate((1, -1)):
            first[n].wait_recv()
            copies.append(send(piece(-to), piece(-to), ag_s.at[i, 2 + n], ag_r.at[i, 2 + n], at_y(to)))
        return copies

    def gather_third(piece, i, second):
        copies = []
        for n, to in enumerate((1, -1)):
            second[n].wait_recv()
            copies.append(send(piece(-2 * to), piece(-2 * to), ag_s.at[i, 4 + n], ag_r.at[i, 4 + n], at_y(to)))
        over = piece(-2 * side)
        return copies + [send(over, over, ag_s.at[i, 6], ag_r.at[i, 6], at_y(2 * side))]

    def ring_third(piece, i, second):
        copies = []
        for n, to in enumerate((1, -1)):
            second[n].wait_recv()
            copies.append(send(piece(-2 * to), piece(-2 * to), ag_s.at[i, 4 + n], ag_r.at[i, 4 + n], at_y(to)))
        return copies

    def ring_fourth(piece, i, third):
        settle(third)
        last = piece(-3 * side)
        return [send(last, last, ag_s.at[i, 6], ag_r.at[i, 6], at_y(side))]

    def share(half, i, far):
        settle(far)
        return send(half, half, fw_s.at[i], fw_r.at[i], mate)

    def spread_top(s):
        @pl.when(p == s)
        def _():
            tsrc[s] = jnp.concatenate([a[0, k].T for k in range(KB)], axis=0).reshape(ST, 2, NY, SL, W)
            for t in range(2 * NY):
                src, dst = tsrc.at[s, :, t % 2, t // 2], tt.at[s, :, t % 2, t // 2]
                if t == s:
                    tt[s, :, t % 2, t // 2] = tsrc[s, :, t % 2, t // 2]
                else:
                    pltpu.make_async_remote_copy(src_ref=src, dst_ref=dst, send_sem=ts_s.at[s, t], recv_sem=ts_r.at[s],
                                                 device_id=(t, q), device_id_type=MESH).start()

    def gather_top(s):
        here = tt.at[s, :, c, y]

        @pl.when(p != s)
        def _():
            pltpu.make_async_remote_copy(src_ref=here, dst_ref=here, send_sem=ts_s.at[s, 0], recv_sem=ts_r.at[s],
                                         device_id=mate, device_id_type=MESH).wait_recv()
        return gather_first(top_piece(s), 3 * s + 2)

    def swap(s, j, tops):
        mask = onehot(j, piv_ref[s:s + 1, :])
        taken = jnp.sum(jnp.where(mask, 1.0, 0.0), axis=1, keepdims=True) > 0.0
        hot = as_hot(mask)
        new = []
        for k in range(KB):
            hi, lo = split(tops[k * W:(k + 1) * W])
            new.append(jnp.where(taken, dot(hot, hi, 1, 1) + dot(hot, lo, 1, 1), a[j, k]))
        return new

    def below(s, j):
        return split(lg[s, W:, :] if j else jnp.where(p > s, lg[s, :W, :], 0.0))

    def update(j):
        new = swap(0, j, tt[0].reshape(KB * W, W))
        low = below(0, j)
        upper = ut[0].reshape(KB * W, W)
        for k in range(KB):
            a[j, k] = new[k] - dot3(low, split(upper[k * W:(k + 1) * W]))

    lined = jnp.logical_or(q == HOLDERS[0], q == HOLDERS[1])

    def rows_first():
        @pl.when(lined)
        def _():
            hot = [as_hot(onehot(j, piv_ref[1:2, :])) for j in range(2)]
            total = jnp.zeros((W, W), jnp.float32)
            for j in range(2):
                for part in split(loc[j * W:(j + 1) * W, :]):
                    total = total + dot(hot[j], part, 0, 0)
            et[...] = total.reshape(2, NY, PR, W)
            remote(et.at[1 - c], ep, e_s.at[0], e_r.at[0], mate).start()

            @pl.when(p == 1)
            def _():
                for t in range(2 * NY):
                    piece = pl.ds((t % 2) * NY * PR + (t // 2) * PR, PR)
                    if t == 1:
                        ms[1] = loc[piece, :]
                    else:
                        remote(loc.at[piece], ms.at[1], n_s.at[t], n_r, (t, q)).start()

    def rows_second():
        @pl.when(lined)
        def _():
            remote(et.at[1 - c], ep, e_s.at[0], e_r.at[0], mate).wait_recv()
            es[...] = et[c] + ep[...]
            for i in range(1, NY):
                remote(es.at[chip(i)], er.at[i - 1], e_s.at[i], e_r.at[i], at_y(i)).start()

    def rows_third():
        @pl.when(lined)
        def _():
            total = es[y]
            for i in range(1, NY):
                remote(es.at[chip(i)], er.at[i - 1], e_s.at[i], e_r.at[i], at_y(i)).wait_recv()
                total = total + er[i - 1]
            ms[0] = total

            @pl.when(p != 1)
            def _():
                remote(ms.at[1], ms.at[1], n_s.at[0], n_r, mate).wait_recv()
        for n in range(2):
            @pl.when(q == HOLDERS[n])
            def _():
                mr[n] = ms[...]
                for i in range(1, NX):
                    remote(mr.at[n], mr.at[n], m_s.at[i], m_r.at[n], at_x(i)).start()

    def rows_fourth():
        for n in range(2):
            @pl.when(z == HOLDERS[n] % NZ)
            def _():
                @pl.when(q != HOLDERS[n])
                def _():
                    remote(mr.at[n], mr.at[n], m_s.at[0], m_r.at[n], mate).wait_recv()
                for i in range(1, NZ):
                    remote(mr.at[n], mr.at[n], m_s.at[NX + i], m_r.at[n], at_z(i)).start()

    def rows_here():
        for n in range(2):
            @pl.when(z != HOLDERS[n] % NZ)
            def _():
                remote(mr.at[n], mr.at[n], m_s.at[0], m_r.at[n], mate).wait_recv()
        mn[:, c, y] = jnp.where(own_ref[0] == HOLDERS[0], mr[0], mr[1])

    def rows_piece(step):
        return mn.at[:, c, chip(step)]

    def rows_near(i):
        return [send(rows_piece(0), rows_piece(0), ag_s.at[i, n], ag_r.at[i, n], at_y(to))
                for n, to in enumerate((2, -2, 1, -1))]

    def rows_far(i, near):
        copies = near[2:]
        for n, to in enumerate((1, -1)):
            near[n].wait_recv()
            piece = rows_piece(-2 * to)
            copies.append(send(piece, piece, ag_s.at[i, 4 + n], ag_r.at[i, 4 + n], at_y(to)))
        over = rows_piece(-2 * side)
        return copies + [send(over, over, ag_s.at[i, 6], ag_r.at[i, 6], at_y(2 * side))]

    every = [(s, h) for s in range(2) for h in range(ST)]
    slot = {(s, h): 3 * s + h for s, h in every}

    pairs = {(0, h): pair_up(0, h) for h in range(ST)}
    rows_first()

    first = jnp.broadcast_to(piv_ref[0:1, :].astype(jnp.float32), (W, W)).T
    hit = jnp.where(first == piv_ref[1:2, :].astype(jnp.float32), 1.0, 0.0)
    place = jnp.sum(hit * lax.broadcasted_iota(jnp.int32, (W, W), 0).astype(jnp.float32), axis=0, keepdims=True)
    moved = jnp.sum(hit, axis=0, keepdims=True) > 0.0
    pt[1] = pick(jnp.where(moved, place.astype(jnp.int32), piv_ref[1:2, :]))
    pairs.update({(1, h): pair_up(1, h) for h in range(ST)})

    rows_second()
    work = {k: reduce_first(*k, pairs[k]) for k in every}
    for n in range(len(HOLDERS)):
        scatter(n)
    for s in range(2):
        spread_top(s)
    rows_third()
    work = {k: reduce_second(*k, work[k]) for k in every}
    rows_fourth()
    for n in range(len(HOLDERS)):
        arrived(n)
    z_copies = [gather_z(i) for i in range(2)]
    work = {k: reduce_third(*k, work[k]) for k in every}
    tops = [gather_top(s) for s in range(2)]
    upper = {}
    for k in every:
        solve(*k, work[k])
        upper[k] = gather_first(upper_piece(*k), slot[k])
    rows_here()
    rows = rows_near(6)
    tops = [gather_second(top_piece(s), 3 * s + 2, tops[s]) for s in range(2)]
    upper = {k: gather_second(upper_piece(*k), slot[k], upper[k]) for k in every}
    x_copies = []
    settle(z_copies[0])
    x_copies.append(gather_x(0))
    rows = rows_far(6, rows)
    tops = [ring_third(top_piece(s), 3 * s + 2, tops[s]) for s in range(2)]
    upper = {k: gather_third(upper_piece(*k), slot[k], upper[k]) for k in every}
    tops = [ring_fourth(top_piece(s), 3 * s + 2, tops[s]) for s in range(2)]
    settle(z_copies[1])
    x_copies.append(gather_x(1))
    rows = share(mn.at[:, c], 6, rows)
    upper = {k: share(ut.at[k[0], k[1], c], slot[k], upper[k]) for k in every}
    tops = [share(tt.at[s, :, c], 3 * s + 2, tops[s]) for s in range(2)]

    for h in range(ST):
        upper[0, h].wait_recv()
    solved = [split(ut[0, h].reshape(WIDE, W)) for h in range(ST)]
    rows.wait_recv()
    mixed = split(lax.dot_general(inv_ref[1], mn[0].reshape(W, W), (((1,), (0,)), ((), ())),
                                  precision=lax.Precision.HIGHEST, preferred_element_type=jnp.float32))
    drop = [dot3(solved[h], mixed) for h in range(ST)]
    second = split(mn[1].reshape(W, W))
    drop_top = [dot3(solved[h], second) for h in range(ST)]
    settle(x_copies[0])
    tops[0].wait_recv()
    for j in range(2):
        update(j)

    @pl.when(p == 0)
    def _():
        whole = ut[0].reshape(KB * W, W)
        for k in range(KB):
            a[0, k] = whole[k * W:(k + 1) * W].T

    ids = lax.broadcasted_iota(jnp.int32, (W, W), 1) + W
    link = first == ids.astype(jnp.float32)
    linked = jnp.sum(jnp.where(link, 1.0, 0.0), axis=0, keepdims=True) > 0.0
    link = as_hot(link)
    tops[1].wait_recv()
    for h in range(ST):
        hi, lo = split(tt[0, h].reshape(WIDE, W))
        raw = jnp.where(linked, dot(hi, link, 1, 0) + dot(lo, link, 1, 0), tt[1, h].reshape(WIDE, W))
        t1[h * WIDE:(h + 1) * WIDE, :] = raw - drop_top[h]
    for j in range(2):
        for k, block in enumerate(swap(1, j, t1[...])):
            o_buf[j, k] = block
    settle(x_copies[1])
    low = [below(1, j) for j in range(2)]
    stores = []

    def finish(k):
        @pl.when(p == 1)
        def _():
            o_buf[0, k] = u1[k * W:(k + 1) * W, :].T
        stores.append(pltpu.make_async_copy(o_buf.at[:, k], o_hbm.at[:, k], out_sem.at[k]))
        stores[-1].start()

    for h in range(ST):
        upper[1, h].wait_recv()
        solved1 = ut[1, h].reshape(WIDE, W) - drop[h]
        u1[h * WIDE:(h + 1) * WIDE, :] = solved1
        solved1 = split(solved1)
        for j in range(2):
            product = dot3(low[j], solved1)
            at = h * (W // 2)
            part = pl.ds(at, W // 2)
            o_buf[j, 2 * h] = o_buf[j, 2 * h] - product[:, at:at + W]
            rest = product[:, :W // 2] if h else product[:, W:]
            o_buf[j, 1, :, part] = o_buf[j, 1, :, part] - rest
        if h == 0:
            finish(0)

    finish(1)
    finish(2)
    for copy in sent:
        copy.wait_send()
    for s in range(2):
        @pl.when(p == s)
        def _():
            for t in range(2 * NY):
                if t != s:
                    piece = tsrc.at[s, :, t % 2, t // 2]
                    pltpu.make_async_remote_copy(src_ref=piece, dst_ref=piece, send_sem=ts_s.at[s, t],
                                                 recv_sem=ts_r.at[s], device_id=mate, device_id_type=MESH).wait_send()
    for n, h in enumerate(HOLDERS):
        @pl.when(q == h)
        def _():
            @pl.loop(1, NQ)
            def _(i):
                piece = loc.at[pl.ds(0, PR)]
                pltpu.make_async_remote_copy(src_ref=piece, dst_ref=piece, send_sem=sc_s.at[i], recv_sem=sc_r.at[n],
                                             device_id=mate, device_id_type=MESH).wait_send()

    @pl.when(lined)
    def _():
        remote(et.at[1 - c], ep, e_s.at[0], e_r.at[0], mate).wait_send()
        for i in range(1, NY):
            remote(es.at[chip(i)], er.at[i - 1], e_s.at[i], e_r.at[i], at_y(i)).wait_send()

        @pl.when(p == 1)
        def _():
            for t in range(2 * NY):
                if t != 1:
                    remote(loc.at[pl.ds(0, PR)], ms.at[1], n_s.at[t], n_r, mate).wait_send()

    for n in range(2):
        @pl.when(q == HOLDERS[n])
        def _():
            for i in range(1, NX):
                remote(mr.at[n], mr.at[n], m_s.at[i], m_r.at[n], mate).wait_send()

        @pl.when(z == HOLDERS[n] % NZ)
        def _():
            for i in range(1, NZ):
                remote(mr.at[n], mr.at[n], m_s.at[NX + i], m_r.at[n], mate).wait_send()
    for copy in stores:
        copy.wait()


def body(matrix, lower_panel, inverses, pivots, panel_owner):
    f32 = jnp.float32
    dma = pltpu.SemaphoreType.DMA
    blocks = matrix.transpose(0, 2, 1, 3)
    any_spec = pl.BlockSpec(memory_space=pl.ANY)
    line = (ST, 2, NY, SL, W)
    out = pl.pallas_call(
        kernel,
        out_shape=jax.ShapeDtypeStruct(blocks.shape, f32),
        in_specs=[any_spec] * 5,
        out_specs=any_spec,
        scratch_shapes=[
            pltpu.VMEM((2, KB, W, W), f32),
            pltpu.VMEM((2 * W, W), f32),
            pltpu.VMEM((2, W, W), f32),
            pltpu.VMEM((2, W), jnp.int32),
            pltpu.SMEM((2,), jnp.int32),
            pltpu.VMEM((2,) + line, f32),
            pltpu.VMEM((2, ST, NY, SL, W), f32),
            pltpu.VMEM((2, ST, NY, SL, W), f32),
            pltpu.VMEM((2, ST, 3, SL, W), f32),
            pltpu.VMEM((2, ST, 2, SL, W), f32),
            pltpu.VMEM((2, ST, 2, SL, W), f32),
            pltpu.VMEM((2, ST, 2, SL, W), f32),
            pltpu.VMEM((2, ST, 2, SL, W), f32),
            pltpu.VMEM((2,) + line, f32),
            pltpu.VMEM((2,) + line, f32),
            pltpu.VMEM((2,) + line, f32),
            pltpu.VMEM((3, PR, W), f32),
            pltpu.VMEM((2, 2 * W, W), f32),
            pltpu.VMEM((2, NY, PR, W), f32),
            pltpu.VMEM((NY, PR, W), f32),
            pltpu.VMEM((NY, PR, W), f32),
            pltpu.VMEM((NY - 1, PR, W), f32),
            pltpu.VMEM((2, PR, W), f32),
            pltpu.VMEM((2, 2, PR, W), f32),
            pltpu.VMEM((2, 2, NY, PR, W), f32),
            pltpu.VMEM((KB * W, W), f32),
            pltpu.VMEM((KB * W, W), f32),
            pltpu.VMEM((2, KB, W, W), f32),
            dma((4 + KB,)), dma((KB,)),
            dma((2, ST)), dma((2, ST)),
            dma((2, ST, 7)), dma((2, ST, 7)),
            dma((2, 2 * NY)), dma((2,)),
            dma((7, 7)), dma((7, 7)),
            dma((7,)), dma((7,)),
            dma((NQ,)), dma((3,)),
            dma((2, NZ)), dma((2, NZ)),
            dma((2, NX)), dma((2, NX)),
            dma((NY,)), dma((NY,)),
            dma((2 * NY,)), dma(()),
            dma((NX + NZ,)), dma((2,)),
        ],
        compiler_params=pltpu.CompilerParams(collective_id=0, has_side_effects=True, vmem_limit_bytes=60 * 2**20),
    )(blocks, lower_panel.reshape(2 * W, W), inverses, pivots, panel_owner)
    return out.transpose(0, 2, 1, 3)


def solution(mesh):
    in_specs = (P(None, "prow", None, "pcol"), P(None, "prow", "pcol"), P(), P(), P())
    return jax.shard_map(body, mesh=mesh, in_specs=in_specs, out_specs=P(None, "prow", None, "pcol"), check_vma=False)
```
